256 devices in a mesh: depth: 2 (over y_lo), row: 16 (over z, core), col: 8 (over x, y_hi).
Axes of the slice: x: 4, y: 4 (y_hi: 2, y_lo: 2; y = y_hi * 2 + y_lo), z: 8, core: 2. Of those that a mesh axis runs over, the one named last changes fastest.
Arguments:
- tokens: bfloat16 [1024, 6144], P(('depth', 'col'), 'row'), may hold values from -6 to 6
- w_in: bfloat16 [6144, 24576], P('row', 'col'), may hold values from -0.078125 to 0.078125
- w_out: bfloat16 [24576, 6144], P('col', 'row'), may hold values from -0.0390625 to 0.0390625
- saved: bfloat16 [1024, 24576], P(('depth', 'row'), 'col'), may hold values from -6 to 6
- grad_out: bfloat16 [1024, 6144], P(('depth', 'col'), 'row'), may hold values from -6 to 6
Outputs:
- grad_tokens: bfloat16 [1024, 6144], P(('depth', 'col'), 'row')
- grad_w_in: bfloat16 [6144, 24576], P('row', 'col')
- grad_w_out: bfloat16 [24576, 6144], P('col', 'row')
The draws below stay inside these ranges and needn't reach their ends.
All inputs are finite; a program needn't handle non-finite values.
Results may differ from the reference program's by a relative error of at most 0.017.
Values may be sent and summed in bfloat16 or wider, within the bound.
A program may use at most 128 MiB of HBM per device.

```python
import math
import jax
import jax.numpy as jnp
from jax import lax

D = 6144
FF = 24576
TOKENS = 1024


def levels(key, shape, split, smallest, largest):
    gain = 1.0
    for axis_at, blocks in split:
        heights = jax.random.uniform(jax.random.fold_in(jax.random.fold_in(key, 6), axis_at), (blocks,), jnp.float32, smallest / len(split), largest / len(split))
        gain = gain * jnp.repeat(jnp.exp(heights), shape[axis_at] // blocks).reshape((-1,) + (1,) * (len(shape) - 1 - axis_at))
    return gain


def noise(stream_key, extent, scale, reach, split=(), dtype=jnp.bfloat16):
    level = levels(stream_key, extent, split, -0.22, 0.18) if split else 1.0
    result = jax.random.normal(stream_key, extent, jnp.float32) * scale * level
    return jnp.minimum(jnp.maximum(result, -reach), reach).astype(dtype)


def setup_inputs(seed: int = 0) -> dict:
    key_of = jax.random.split(jax.random.key(seed), 6)
    tokens = noise(key_of[0], (TOKENS, D), 1.0, 6.0, ((0, 16), (1, 16)))
    w_in = noise(key_of[1], (D, FF), D ** -0.5, 0.078125, ((0, 16), (1, 8)))
    w_out = noise(key_of[2], (FF, D), FF ** -0.5, 0.0390625, ((0, 8), (1, 16)))
    saved = noise(key_of[3], (TOKENS, FF), 1.0, 6.0, ((0, 32), (1, 8)))
    grad_out = noise(key_of[4], (TOKENS, D), 1.0, 6.0, ((0, 16), (1, 16)))
    return dict(tokens=tokens, w_in=w_in, w_out=w_out, saved=saved, grad_out=grad_out)


def gelu_parts(values):
    normal_cdf = 0.5 * (1.0 + jax.scipy.special.erf(values / math.sqrt(2.0)))
    normal_pdf = jnp.exp(-0.5 * values * values) / math.sqrt(2.0 * math.pi)
    return (values * normal_cdf, normal_cdf + values * normal_pdf)

def reference(tokens, w_in, w_out, saved, grad_out):
    contract_last = (((1,), (1,)), ((), ()))
    contract_first = (((0,), (0,)), ((), ()))
    act_full, gelu_slope = gelu_parts(saved.astype(jnp.float32))
    act = act_full.astype(jnp.bfloat16)
    act_grad = lax.dot_general(grad_out, w_out, contract_last, preferred_element_type=jnp.float32)
    hidden_grad = (act_grad * gelu_slope).astype(jnp.bfloat16)
    grad_tokens = lax.dot_general(hidden_grad, w_in, contract_last, preferred_element_type=jnp.float32).astype(jnp.bfloat16)
    grad_w_in = lax.dot_general(tokens, hidden_grad, contract_first, preferred_element_type=jnp.float32).astype(jnp.bfloat16)
    grad_w_out = lax.dot_general(act, grad_out, contract_first, preferred_element_type=jnp.float32).astype(jnp.bfloat16)
    return (grad_tokens, grad_w_in, grad_w_out)
```

```python
import functools
import math

import jax
import jax.numpy as jnp
from jax import lax
from jax.experimental import pallas as pl
from jax.experimental.pallas import tpu as pltpu
from jax.sharding import PartitionSpec as P

F32, BF16 = jnp.float32, jnp.bfloat16
MESH = pl.DeviceIdType.MESH

CHUNKS = 6
QUARTER = 768
WIDTH = QUARTER // CHUNKS
HALF = 384
FEATURES = 768
TOKENS = 1024
RS_START = 4
SLOTS = RS_START + 8 + CHUNKS

LAST_LAST = (((1,), (1,)), ((), ()))
PLAIN = (((1,), (0,)), ((), ()))


def dot(a, b, dims):
    return lax.dot_general(a, b, dims, preferred_element_type=F32)


def ds(start, size):
    return pl.ds(pl.multiple_of(start, size), size)


def kernel(
    tokens, w_in, w_out, saved, grad_out,
    grad_tokens, grad_w_in, grad_w_out,
    saved_q, up, inp, inp_t, wo, wi, act_t, hid, slope, part,
    rs_out, rs_in, dwo, dwi, tail, sib_out, sib_in,
    x_out, x_in, fin, y_out, y_in,
    local_sem, start_send, start_recv, up_send, up_recv, inp_send, inp_recv,
    act_send, act_recv, rs_send, rs_recv, hid_send, hid_recv,
    dw_local, dw_send, dw_recv, sib_send, sib_recv, x_send, x_recv, y_send, y_recv,
):
    depth, row, col = lax.axis_index("depth"), lax.axis_index("row"), lax.axis_index("col")
    z, core = lax.div(row, 2), lax.rem(row, 2)
    x, y_hi = lax.div(col, 2), lax.rem(col, 2)
    y = y_hi * 2 + depth
    other = 1 - core
    quarter = depth * 2 + core

    def at_y(v):
        v = lax.rem(v + 4, 4)
        return (lax.rem(v, 2), row, x * 2 + lax.div(v, 2))

    def at_x(v):
        return (depth, row, lax.rem(v + 4, 4) * 2 + y_hi)

    def at_z(v):
        return (depth, lax.rem(v + 8, 8) * 2 + core, col)

    to_z = (at_z(z + 1), at_z(z - 1))
    to_x = (at_x(x + 1), at_x(x - 1))
    to_y = (at_y(y + 1), at_y(y - 1))
    sibling = (depth, z * 2 + other, col)
    partner = (1 - depth, row, col)
    diagonal = (1 - depth, z * 2 + other, col)

    def send(src, dst, send_sem, recv_sem, device):
        return pltpu.make_async_remote_copy(
            src_ref=src, dst_ref=dst, send_sem=send_sem, recv_sem=recv_sem,
            device_id=device, device_id_type=MESH,
        )

    mine = ds(core * HALF, HALF)

    own_rows = ds(x * 256 + y * 64, 64)
    locals_ = [
        pltpu.make_async_copy(saved.at[:, ds(quarter * QUARTER, QUARTER)], saved_q.at[quarter], local_sem.at[0]),
        pltpu.make_async_copy(grad_out, up.at[own_rows, mine], local_sem.at[1]),
        pltpu.make_async_copy(tokens, inp.at[own_rows, mine], local_sem.at[2]),
        pltpu.make_async_copy(w_out.at[ds(quarter * QUARTER, QUARTER), :], wo.at[:, mine], local_sem.at[3]),
        pltpu.make_async_copy(w_in.at[:, ds(quarter * QUARTER, QUARTER)], wi.at[mine, :], local_sem.at[4]),
    ]
    for copy in locals_:
        copy.start()
    barrier = pltpu.get_barrier_semaphore()
    for device in (*to_z, *to_x, *to_y, sibling, diagonal):
        pl.semaphore_signal(barrier, inc=1, device_id=device, device_id_type=MESH)
    pl.semaphore_wait(barrier, 8)

    sib_quarter = depth * 2 + other
    starts = []
    for i, (device, q) in enumerate((
        (sibling, sib_quarter),
        (partner, (1 - depth) * 2 + core),
        (diagonal, (1 - depth) * 2 + other),
    )):
        starts.append(send(
            saved.at[:, ds(q * QUARTER, QUARTER)], saved_q.at[quarter],
            start_send.at[i], start_recv.at[i], device,
        ))
    starts.append(send(
        w_out.at[ds(sib_quarter * QUARTER, QUARTER), :], wo.at[:, mine],
        start_send.at[3], start_recv.at[3], sibling,
    ))
    starts.append(send(
        w_in.at[:, ds(sib_quarter * QUARTER, QUARTER)], wi.at[mine, :],
        start_send.at[4], start_recv.at[4], sibling,
    ))

    def gather(source, buf, send_sem, recv_sem):
        def place(v_x, v_y):
            return lax.rem(v_x + 4, 4) * 256 + lax.rem(v_y + 4, 4) * 64

        def block(i, rows, size, device):
            ref = buf.at[ds(rows, size), mine]
            return send(ref, ref, send_sem.at[i], recv_sem.at[i], device)

        own = buf.at[own_rows, mine]
        y0 = send(source, own, send_sem.at[0], recv_sem.at[0], to_y[0])
        y1 = send(source, own, send_sem.at[1], recv_sem.at[1], to_y[1])
        y2 = block(2, place(x, y - 1), 32, to_y[0])
        y3 = block(3, place(x, y + 1) + 32, 32, to_y[1])
        group = lambda v: lax.rem(v + 4, 4) * 256
        x0 = block(4, group(x), 256, to_x[0])
        x1 = block(5, group(x), 256, to_x[1])
        x2 = block(6, group(x - 1), 128, to_x[0])
        x3 = block(7, group(x + 1) + 128, 128, to_x[1])
        s = [block(8 + i, group(x + o), 256, sibling) for i, o in enumerate((0, -1, 1, 2))]
        return y0, y1, y2, y3, x0, x1, x2, x3, *s

    up_copies = gather(grad_out, up, up_send, up_recv)
    inp_copies = gather(tokens, inp, inp_send, inp_recv)

    for copy in starts[:3]:
        copy.start()
    for copy in up_copies[:2]:
        copy.start()
    for copy in inp_copies[:2]:
        copy.start()
    for copy in starts[3:]:
        copy.start()
    for copy in locals_:
        copy.wait()
    for copy in starts[:3]:
        copy.wait_recv()

    def gather_step(copies, stage):
        y0, y1, y2, y3, x0, x1, x2, x3, s0, s1, s2, s3 = copies
        if stage == 0:
            y0.wait_recv()
            y2.start()
            y1.wait_recv()
            y3.start()
        if stage == 1:
            y2.wait_recv()
            y3.wait_recv()
            x0.start()
            x1.start()
            s0.start()
        if stage == 2:
            x0.wait_recv()
            x2.start()
            s1.start()
            x1.wait_recv()
            x3.start()
            s2.start()
        if stage == 3:
            x2.wait_recv()
            x3.wait_recv()
            s3.start()
        if stage == 4:
            for copy in (s0, s1, s2, s3):
                copy.wait_recv()

    def act_copy(j, s, way):
        token_block = ds(lax.rem(z + (8 - s if way == 0 else s), 8) * 128, 128)
        if s == 3:
            rows = pl.ds(way * (WIDTH // 2), WIDTH // 2)
        else:
            rows = pl.ds(0, WIDTH)
        ref = act_t.at[j, rows, token_block]
        return send(ref, ref, act_send.at[j, s, way], act_recv.at[j, s, way], to_z[way])

    def hid_copy(j, s, way):
        start = lax.rem(z + (8 - s if way == 0 else s), 8) * 128
        if s == 3:
            ref = hid.at[j, ds(start + way * 64, 64), :]
        else:
            ref = hid.at[j, ds(start, 128), :]
        return send(ref, ref, hid_send.at[j, s, way], hid_recv.at[j, s, way], to_z[way])

    def rs_copy(j, s, way):
        rows = pl.ds(way * 64, 64) if s == 0 else pl.ds(0, 128)
        return send(
            rs_out.at[j, s, way, rows, :], rs_in.at[j, s, way, rows, :],
            rs_send.at[j, s, way], rs_recv.at[j, s, way], to_z[way],
        )

    def dw_copies(which, j):
        if which == 0:
            place = grad_w_out.at[ds(quarter * QUARTER + j * WIDTH, WIDTH), :]
            blocks = dwo
        else:
            place = grad_w_in.at[:, ds(quarter * QUARTER + j * WIDTH, WIDTH)]
            blocks = dwi
        here = pltpu.make_async_copy(blocks.at[j, core], place, dw_local.at[which, j])
        there = [
            send(blocks.at[j, half], place, dw_send.at[which, j, i], dw_recv.at[which, j, i], device)
            for i, (device, half) in enumerate(((partner, core), (diagonal, other), (sibling, other)))
        ]
        return here, there

    def slot(t, carry):
        def when(j):
            return pl.when(jnp.logical_and(j >= 0, j < CHUNKS))

        @pl.when(t < CHUNKS)
        def _():
            values = saved_q[:, :, ds(t * WIDTH, WIDTH)].reshape(128, WIDTH).astype(F32)
            cdf = 0.5 * (1.0 + lax.erf(values / math.sqrt(2.0)))
            pdf = jnp.exp(-0.5 * values * values) / math.sqrt(2.0 * math.pi)
            slope[t] = cdf + values * pdf
            act_t[t, :, ds(z * 128, 128)] = (values * cdf).T.astype(BF16)
            for way in range(2):
                act_copy(t, 0, way).start()

        for s in range(1, 4):
            @when(t - s)
            def _():
                for way in range(2):
                    act_copy(t - s, s - 1, way).wait_recv()
                    act_copy(t - s, s, way).start()

        for stage in range(5):
            @pl.when(t == stage)
            def _():
                gather_step(up_copies, stage)

        for stage, at in enumerate((0, 2, 3, 4, 5)):
            @pl.when(t == at)
            def _():
                gather_step(inp_copies, stage)

        @pl.when(t == RS_START)
        def _():
            starts[3].wait_recv()

        first = t - RS_START

        @when(first)
        def _():
            j = first
            part[j] = dot(up[...], wo[ds(j * WIDTH, WIDTH), :], LAST_LAST)
            block = lax.rem(z + 4, 8) * 128
            for way in range(2):
                rows = pl.ds(way * 64, 64)
                rs_out[j, 0, way, rows, :] = part[j, ds(block + way * 64, 64), :].astype(BF16)
                rs_copy(j, 0, way).start()

        for s in range(1, 4):
            @when(first - s)
            def _():
                j = first - s
                for way in range(2):
                    rs_copy(j, s - 1, way).wait_recv()
                    block = lax.rem(z + (4 - s if way == 0 else 4 + s), 8) * 128
                    if s == 1:
                        near, far = pl.ds(way * 64, 64), pl.ds((1 - way) * 64, 64)
                        rs_out[j, s, way, near, :] = (
                            part[j, ds(block + way * 64, 64), :] + rs_in[j, 0, way, near, :].astype(F32)
                        ).astype(BF16)
                        rs_out[j, s, way, far, :] = part[j, ds(block + (1 - way) * 64, 64), :].astype(BF16)
                    else:
                        rs_out[j, s, way] = (
                            part[j, ds(block, 128), :] + rs_in[j, s - 1, way].astype(F32)
                        ).astype(BF16)
                    rs_copy(j, s, way).start()

        second = first - 4

        @when(second)
        def _():
            j = second
            for way in range(2):
                rs_copy(j, 3, way).wait_recv()
            mine_z = ds(z * 128, 128)
            total = part[j, mine_z, :] + rs_in[j, 3, 0].astype(F32) + rs_in[j, 3, 1].astype(F32)
            hid[j, mine_z, :] = (total * slope[j]).astype(BF16)
            for way in range(2):
                hid_copy(j, 0, way).start()

        for s in range(1, 4):
            @when(second - s)
            def _():
                for way in range(2):
                    hid_copy(second - s, s - 1, way).wait_recv()
                    hid_copy(second - s, s, way).start()

        @when(t - 4)
        def _():
            j = t - 4
            for way in range(2):
                act_copy(j, 3, way).wait_recv()
            out = dot(act_t[j], up[...], PLAIN).astype(BF16)
            dwo[j, 0] = out[:, :HALF]
            dwo[j, 1] = out[:, HALF:]
            here, there = dw_copies(0, j)
            for copy in there:
                copy.start()
            here.start()

        @when(t - 6)
        def _():
            j = t - 6
            for i in range(FEATURES // 128 // CHUNKS if CHUNKS < 6 else 1):
                columns = (j * (6 // CHUNKS) + i) * 128
                inp_t[ds(columns, 128), :] = inp[:, ds(columns, 128)].astype(F32).T.astype(BF16)

        @when(second - 4)
        def _():
            j = second - 4
            for way in range(2):
                hid_copy(j, 3, way).wait_recv()
            for half in range(2):
                dwi[j, half] = dot(inp_t[pl.ds(half * HALF, HALF), :], hid[j], PLAIN).astype(BF16)
            here, there = dw_copies(1, j)
            for copy in there:
                copy.start()
            here.start()

        return carry

    lax.fori_loop(0, SLOTS, slot, 0)

    starts[4].wait_recv()
    order = (2, 1, 3, 0)

    def sib_copy(i):
        return send(sib_out.at[i], sib_in.at[i], sib_send.at[i], sib_recv.at[i], sibling)

    def partial(i, carry):
        ahead = jnp.where(i == 0, 2, jnp.where(i == 1, 1, jnp.where(i == 2, 3, 0)))
        rows = ds(lax.rem(x + ahead, 4) * 256, 256)
        for half in range(2):
            features = pl.ds(half * HALF, HALF)
            total = dot(hid[0, rows, :], wi[features, pl.ds(0, WIDTH)], LAST_LAST)
            for j in range(1, CHUNKS):
                total += dot(hid[j, rows, :], wi[features, pl.ds(j * WIDTH, WIDTH)], LAST_LAST)
            tail[i, half] = total
        sib_out[i] = tail[i, other].astype(BF16)
        sib_copy(i).start()
        return carry

    lax.fori_loop(0, 4, partial, 0)

    def chip_sum(i, rows):
        return tail[i, core, rows, :] + sib_in[i, rows, :].astype(F32)

    everything = pl.ds(0, 256)

    def x_copy(s, way):
        rows = pl.ds(way * 128, 128) if s == 0 else everything
        return send(
            x_out.at[s, way, rows, :], x_in.at[s, way, rows, :],
            x_send.at[s, way], x_recv.at[s, way], to_x[way],
        )

    sib_copy(0).wait_recv()
    for way in range(2):
        rows = pl.ds(way * 128, 128)
        x_out[0, way, rows, :] = chip_sum(0, rows).astype(BF16)
        x_copy(0, way).start()
    for way in range(2):
        sib_copy(1 + way).wait_recv()
        near, far = pl.ds(way * 128, 128), pl.ds((1 - way) * 128, 128)
        x_out[1, way, far, :] = chip_sum(1 + way, far).astype(BF16)
        x_copy(0, way).wait_recv()
        x_out[1, way, near, :] = (chip_sum(1 + way, near) + x_in[0, way, near, :].astype(F32)).astype(BF16)
        x_copy(1, way).start()
    sib_copy(3).wait_recv()
    fin[...] = chip_sum(3, everything)
    for way in range(2):
        x_copy(1, way).wait_recv()
        fin[...] += x_in[1, way].astype(F32)

    def y_copy(s, way):
        rows = pl.ds(way * 32, 32) if s == 0 else pl.ds(0, 64)
        return send(
            y_out.at[s, way, rows, :], y_in.at[s, way, rows, :],
            y_send.at[s, way], y_recv.at[s, way], to_y[way],
        )

    for way in range(2):
        rows = pl.ds(way * 32, 32)
        y_out[0, way, rows, :] = fin[ds(lax.rem(y + 2, 4) * 64 + way * 32, 32), :].astype(BF16)
        y_copy(0, way).start()
    for way in range(2):
        block = lax.rem(y + (1 if way == 0 else 3), 4) * 64
        near, far = pl.ds(way * 32, 32), pl.ds((1 - way) * 32, 32)
        y_copy(0, way).wait_recv()
        y_out[1, way, far, :] = fin[ds(block + (1 - way) * 32, 32), :].astype(BF16)
        y_out[1, way, near, :] = (
            fin[ds(block + way * 32, 32), :] + y_in[0, way, near, :].astype(F32)
        ).astype(BF16)
        y_copy(1, way).start()
    total = fin[ds(y * 64, 64), :]
    for way in range(2):
        y_copy(1, way).wait_recv()
        total += y_in[1, way].astype(F32)
    grad_tokens[...] = total.astype(BF16)

    for copy in (*starts, *up_copies, *inp_copies):
        copy.wait_send()
    for i in range(4):
        sib_copy(i).wait_send()
    for s in range(2):
        for way in range(2):
            x_copy(s, way).wait_send()
            y_copy(s, way).wait_send()

    def drain(j, carry):
        for s in range(4):
            for way in range(2):
                act_copy(j, s, way).wait_send()
                rs_copy(j, s, way).wait_send()
                hid_copy(j, s, way).wait_send()
        for which in range(2):
            here, there = dw_copies(which, j)
            here.wait()
            for copy in there:
                copy.wait()
        return carry

    lax.fori_loop(0, CHUNKS, drain, 0)


def shards(tokens, w_in, w_out, saved, grad_out):
    any_space = pl.BlockSpec(memory_space=pl.ANY)
    vmem = pl.BlockSpec(memory_space=pltpu.VMEM)
    dma = pltpu.SemaphoreType.DMA
    return pl.pallas_call(
        kernel,
        out_shape=(
            jax.ShapeDtypeStruct(tokens.shape, BF16),
            jax.ShapeDtypeStruct(w_in.shape, BF16),
            jax.ShapeDtypeStruct(w_out.shape, BF16),
        ),
        in_specs=[any_space] * 5,
        out_specs=(vmem, any_space, any_space),
        scratch_shapes=[
            pltpu.VMEM((4, 32, QUARTER), BF16),
            pltpu.VMEM((TOKENS, FEATURES), BF16),
            pltpu.VMEM((TOKENS, FEATURES), BF16),
            pltpu.VMEM((FEATURES, TOKENS), BF16),
            pltpu.VMEM((QUARTER, FEATURES), BF16),
            pltpu.VMEM((FEATURES, QUARTER), BF16),
            pltpu.VMEM((CHUNKS, WIDTH, TOKENS), BF16),
            pltpu.VMEM((CHUNKS, TOKENS, WIDTH), BF16),
            pltpu.VMEM((CHUNKS, 128, WIDTH), F32),
            pltpu.VMEM((CHUNKS, TOKENS, WIDTH), F32),
            pltpu.VMEM((CHUNKS, 4, 2, 128, WIDTH), BF16),
            pltpu.VMEM((CHUNKS, 4, 2, 128, WIDTH), BF16),
            pltpu.VMEM((CHUNKS, 2, WIDTH, HALF), BF16),
            pltpu.VMEM((CHUNKS, 2, HALF, WIDTH), BF16),
            pltpu.VMEM((4, 2, 256, HALF), F32),
            pltpu.VMEM((4, 256, HALF), BF16),
            pltpu.VMEM((4, 256, HALF), BF16),
            pltpu.VMEM((2, 2, 256, HALF), BF16),
            pltpu.VMEM((2, 2, 256, HALF), BF16),
            pltpu.VMEM((256, HALF), F32),
            pltpu.VMEM((2, 2, 64, HALF), BF16),
            pltpu.VMEM((2, 2, 64, HALF), BF16),
            dma((5,)),
            dma((5,)), dma((5,)),
            dma((12,)), dma((12,)),
            dma((12,)), dma((12,)),
            dma((CHUNKS, 4, 2)), dma((CHUNKS, 4, 2)),
            dma((CHUNKS, 4, 2)), dma((CHUNKS, 4, 2)),
            dma((CHUNKS, 4, 2)), dma((CHUNKS, 4, 2)),
            dma((2, CHUNKS)), dma((2, CHUNKS, 3)), dma((2, CHUNKS, 3)),
            dma((4,)), dma((4,)),
            dma((2, 2)), dma((2, 2)),
            dma((2, 2)), dma((2, 2)),
        ],
        compiler_params=pltpu.CompilerParams(
            collective_id=0, has_side_effects=True, vmem_limit_bytes=48 * 2**20
        ),
        name="mlp_backward",
    )(tokens, w_in, w_out, saved, grad_out)


def solution(mesh):
    in_specs = (
        P(("depth", "col"), "row"),
        P("row", "col"),
        P("col", "row"),
        P(("depth", "row"), "col"),
        P(("depth", "col"), "row"),
    )
    out_specs = (P(("depth", "col"), "row"), P("row", "col"), P("col", "row"))
    return jax.shard_map(shards, mesh=mesh, in_specs=in_specs, out_specs=out_specs, check_vma=False)
```

```python
import functools
import math

import jax
import jax.numpy as jnp
from jax import lax
from jax.experimental import pallas as pl
from jax.experimental.pallas import tpu as pltpu
from jax.sharding import PartitionSpec as P

F32, BF16 = jnp.float32, jnp.bfloat16
MESH = pl.DeviceIdType.MESH

CHUNKS = 3
QUARTER = 768
WIDTH = QUARTER // CHUNKS
HALF = 384
FEATURES = 768
TOKENS = 1024
RS_START = 4
SLOTS = RS_START + 8 + CHUNKS
ACT_AT = (0, 1, 2)
UP_AT = (0, 1, 2, 3, 3)
INP_AT = (1, 2, 4, 5, 6, 7)

LAST_LAST = (((1,), (1,)), ((), ()))
PLAIN = (((1,), (0,)), ((), ()))


def dot(a, b, dims):
    return lax.dot_general(a, b, dims, preferred_element_type=F32)


def ds(start, size):
    return pl.ds(pl.multiple_of(start, size), size)


def kernel(
    tokens, w_in, w_out, saved, grad_out,
    grad_tokens, grad_w_in, grad_w_out,
    saved_q, up, inp, inp_t, wo, wi, act_t, hid, slope, part,
    rs_out, rs_in, dwo, dwi, tail, sib_out, sib_in,
    x_out, x_in, fin, y_out, y_in,
    local_sem, start_send, start_recv, up_send, up_recv, inp_send, inp_recv,
    act_send, act_recv, rs_send, rs_recv, hid_send, hid_recv,
    dw_local, dw_send, dw_recv, sib_send, sib_recv, x_send, x_recv, y_send, y_recv,
):
    depth, row, col = lax.axis_index("depth"), lax.axis_index("row"), lax.axis_index("col")
    z, core = lax.div(row, 2), lax.rem(row, 2)
    x, y_hi = lax.div(col, 2), lax.rem(col, 2)
    y = y_hi * 2 + depth
    other = 1 - core
    quarter = depth * 2 + core

    def at_y(v):
        v = lax.rem(v + 4, 4)
        return (lax.rem(v, 2), row, x * 2 + lax.div(v, 2))

    def at_x(v):
        return (depth, row, lax.rem(v + 4, 4) * 2 + y_hi)

    def at_z(v):
        return (depth, lax.rem(v + 8, 8) * 2 + core, col)

    to_z = (at_z(z + 1), at_z(z - 1))
    to_x = (at_x(x + 1), at_x(x - 1))
    to_y = (at_y(y + 1), at_y(y - 1))
    sibling = (depth, z * 2 + other, col)
    partner = (1 - depth, row, col)
    diagonal = (1 - depth, z * 2 + other, col)

    def send(src, dst, send_sem, recv_sem, device):
        return pltpu.make_async_remote_copy(
            src_ref=src, dst_ref=dst, send_sem=send_sem, recv_sem=recv_sem,
            device_id=device, device_id_type=MESH,
        )

    mine = ds(core * HALF, HALF)

    own_rows = ds(x * 256 + y * 64, 64)
    locals_ = [
        pltpu.make_async_copy(saved.at[:, ds(quarter * QUARTER, QUARTER)], saved_q.at[quarter], local_sem.at[0]),
        pltpu.make_async_copy(grad_out, up.at[own_rows, mine], local_sem.at[1]),
        pltpu.make_async_copy(tokens, inp.at[own_rows, mine], local_sem.at[2]),
        pltpu.make_async_copy(w_out.at[ds(quarter * QUARTER, QUARTER), :], wo.at[:, mine], local_sem.at[3]),
        pltpu.make_async_copy(w_in.at[:, ds(quarter * QUARTER, QUARTER)], wi.at[mine, :], local_sem.at[4]),
    ]
    for copy in locals_:
        copy.start()
    barrier = pltpu.get_barrier_semaphore()
    for device in (*to_z, *to_x, *to_y, sibling, diagonal):
        pl.semaphore_signal(barrier, inc=1, device_id=device, device_id_type=MESH)
    pl.semaphore_wait(barrier, 8)

    sib_quarter = depth * 2 + other
    starts = []
    for i, (device, q) in enumerate((
        (sibling, sib_quarter),
        (partner, (1 - depth) * 2 + core),
        (diagonal, (1 - depth) * 2 + other),
    )):
        starts.append(send(
            saved.at[:, ds(q * QUARTER, QUARTER)], saved_q.at[quarter],
            start_send.at[i], start_recv.at[i], device,
        ))
    starts.append(send(
        w_out.at[ds(sib_quarter * QUARTER, QUARTER), :], wo.at[:, mine],
        start_send.at[3], start_recv.at[3], sibling,
    ))
    starts.append(send(
        w_in.at[:, ds(sib_quarter * QUARTER, QUARTER)], wi.at[mine, :],
        start_send.at[4], start_recv.at[4], sibling,
    ))

    def place(d_x, d_y):
        return lax.rem(x + d_x + 4, 4) * 256 + lax.rem(y + d_y + 4, 4) * 64

    def up_copy(i, rows, size, device, src=None):
        ref = up.at[ds(rows, size), mine]
        return send(ref if src is None else src, ref, up_send.at[i], up_recv.at[i], device)

    up_y = (
        up_copy(0, place(0, 0), 64, to_y[0], grad_out),
        up_copy(1, place(0, 0), 64, to_y[1], grad_out),
        up_copy(2, place(0, -1), 32, to_y[0]),
        up_copy(3, place(0, 1) + 32, 32, to_y[1]),
    )
    steps_y = (0, -1, 1, 2)
    up_x = [
        [
            up_copy(4 + 4 * way + k, place(0, d), 64, to_x[way], grad_out if d == 0 else None)
            for k, d in enumerate(steps_y)
        ]
        for way in range(2)
    ]
    up_far = (
        up_copy(12, place(-1, 0), 64, to_x[0]),
        up_copy(13, place(-1, -1), 64, to_x[0]),
        up_copy(14, place(1, 1), 64, to_x[1]),
        up_copy(15, place(1, 2), 64, to_x[1]),
    )
    up_sib = [
        up_copy(16 + i, lax.rem(x + d + 4, 4) * 256, 256, sibling) for i, d in enumerate((0, -1, 1))
    ] + [up_copy(19 + k, place(2, d), 64, sibling) for k, d in enumerate(steps_y)]
    up_copies = (*up_y, *up_x[0], *up_x[1], *up_far, *up_sib)

    def up_step(stage):
        if stage == 0:
            up_y[0].wait_recv()
            up_y[2].start()
            for way in range(2):
                up_x[way][1].start()
            up_y[1].wait_recv()
            up_y[3].start()
            for way in range(2):
                up_x[way][2].start()
            for way in range(2):
                up_x[way][0].wait_recv()
            up_far[0].start()
        if stage == 1:
            for i in (2, 3):
                up_y[i].wait_recv()
            for way in range(2):
                up_x[way][3].start()
            up_sib[0].start()
            for way in range(2):
                up_x[way][1].wait_recv()
                up_x[way][2].wait_recv()
            up_far[1].start()
            up_far[2].start()
        if stage == 2:
            for way in (1, 0):
                up_x[way][3].wait_recv()
                if way == 1:
                    up_far[3].start()
            up_sib[1].start()
            up_sib[2].start()
            up_far[0].wait_recv()
            up_sib[3].start()
        if stage == 3:
            for k in range(1, 4):
                up_far[k].wait_recv()
                up_sib[3 + k].start()
        if stage == 4:
            for copy in up_sib:
                copy.wait_recv()

    def inp_copy(i, rows, size, device, src=None):
        ref = inp.at[ds(rows, size), mine]
        return send(ref if src is None else src, ref, inp_send.at[i], inp_recv.at[i], device)

    group = lambda d: lax.rem(x + d + 4, 4) * 256
    inp_copies = (
        inp_copy(0, place(0, 0), 64, to_y[0], tokens),
        inp_copy(1, place(0, 0), 64, to_y[1], tokens),
        inp_copy(2, place(0, -1), 32, to_y[0]),
        inp_copy(3, place(0, 1) + 32, 32, to_y[1]),
        inp_copy(4, group(0), 256, to_x[0]),
        inp_copy(5, group(0), 256, to_x[1]),
        inp_copy(6, group(-1), 128, to_x[0]),
        inp_copy(7, group(1) + 128, 128, to_x[1]),
        *[inp_copy(8 + i, group(d), 256, sibling) for i, d in enumerate((0, -1, 1, 2))],
    )

    for copy in starts[:3]:
        copy.start()
    for copy in up_y[:2]:
        copy.start()
    for way in range(2):
        up_x[way][0].start()
    for copy in starts[3:]:
        copy.start()
    for copy in locals_:
        copy.wait()
    for copy in starts[:3]:
        copy.wait_recv()

    def inp_step(stage):
        y0, y1, y2, y3, x0, x1, x2, x3, s0, s1, s2, s3 = inp_copies
        if stage == 0:
            y0.start()
            y1.start()
        if stage == 1:
            y0.wait_recv()
            y2.start()
            y1.wait_recv()
            y3.start()
        if stage == 2:
            y2.wait_recv()
            y3.wait_recv()
            x0.start()
            x1.start()
            s0.start()
        if stage == 3:
            x0.wait_recv()
            x2.start()
            s1.start()
            x1.wait_recv()
            x3.start()
            s2.start()
        if stage == 4:
            x2.wait_recv()
            x3.wait_recv()
            s3.start()
        if stage == 5:
            for copy in (s0, s1, s2, s3):
                copy.wait_recv()

    def act_copy(j, s, way):
        token_block = ds(lax.rem(z + (8 - s if way == 0 else s), 8) * 128, 128)
        if s == 3:
            rows = pl.ds(way * (WIDTH // 2), WIDTH // 2)
        else:
            rows = pl.ds(0, WIDTH)
        ref = act_t.at[j, rows, token_block]
        return send(ref, ref, act_send.at[j, s, way], act_recv.at[j, s, way], to_z[way])

    def hid_copy(j, s, way):
        start = lax.rem(z + (8 - s if way == 0 else s), 8) * 128
        if s == 3:
            ref = hid.at[j, ds(start + way * 64, 64), :]
        else:
            ref = hid.at[j, ds(start, 128), :]
        return send(ref, ref, hid_send.at[j, s, way], hid_recv.at[j, s, way], to_z[way])

    def rs_copy(j, s, way):
        rows = pl.ds(way * 64, 64) if s == 0 else pl.ds(0, 128)
        return send(
            rs_out.at[j, s, way, rows, :], rs_in.at[j, s, way, rows, :],
            rs_send.at[j, s, way], rs_recv.at[j, s, way], to_z[way],
        )

    def dw_copies(which, j):
        if which == 0:
            place = grad_w_out.at[ds(quarter * QUARTER + j * WIDTH, WIDTH), :]
            blocks = dwo
        else:
            place = grad_w_in.at[:, ds(quarter * QUARTER + j * WIDTH, WIDTH)]
            blocks = dwi
        here = pltpu.make_async_copy(blocks.at[j, core], place, dw_local.at[which, j])
        there = [
            send(blocks.at[j, half], place, dw_send.at[which, j, i], dw_recv.at[which, j, i], device)
            for i, (device, half) in enumerate(((partner, core), (diagonal, other), (sibling, other)))
        ]
        return here, there

    def act_at(u):
        chunk, valid = 0, u == ACT_AT[0]
        for j in range(1, CHUNKS):
            chunk = jnp.where(u == ACT_AT[j], j, chunk)
            valid = jnp.logical_or(valid, u == ACT_AT[j])
        return chunk, valid

    def slot(t, carry):
        def when(j):
            return pl.when(jnp.logical_and(j >= 0, j < CHUNKS))

        first = t - RS_START
        second = first - 4

        j_act, valid = act_at(t)

        @pl.when(valid)
        def _():
            j = j_act
            values = saved_q[:, :, ds(j * WIDTH, WIDTH)].reshape(128, WIDTH).astype(F32)
            cdf = 0.5 * (1.0 + lax.erf(values / math.sqrt(2.0)))
            pdf = jnp.exp(-0.5 * values * values) / math.sqrt(2.0 * math.pi)
            slope[j] = cdf + values * pdf
            act_t[j, :, ds(z * 128, 128)] = (values * cdf).T.astype(BF16)
            for way in range(2):
                act_copy(j, 0, way).start()

        for s in range(1, 4):
            j_act, valid = act_at(t - s)

            @pl.when(valid)
            def _():
                for way in range(2):
                    act_copy(j_act, s - 1, way).wait_recv()
                    act_copy(j_act, s, way).start()

        @when(first)
        def _():
            j = first
            block = lax.rem(z + 4, 8) * 128
            for way in range(2):
                rows = pl.ds(way * 64, 64)
                rs_out[j, 0, way, rows, :] = part[j, ds(block + way * 64, 64), :].astype(BF16)
                rs_copy(j, 0, way).start()

        for s in range(1, 4):
            @when(first - s)
            def _():
                j = first - s
                for way in range(2):
                    rs_copy(j, s - 1, way).wait_recv()
                    block = lax.rem(z + (4 - s if way == 0 else 4 + s), 8) * 128
                    if s == 1:
                        near, far = pl.ds(way * 64, 64), pl.ds((1 - way) * 64, 64)
                        rs_out[j, s, way, near, :] = (
                            part[j, ds(block + way * 64, 64), :] + rs_in[j, 0, way, near, :].astype(F32)
                        ).astype(BF16)
                        rs_out[j, s, way, far, :] = part[j, ds(block + (1 - way) * 64, 64), :].astype(BF16)
                    else:
                        rs_out[j, s, way] = (
                            part[j, ds(block, 128), :] + rs_in[j, s - 1, way].astype(F32)
                        ).astype(BF16)
                    rs_copy(j, s, way).start()

        @when(second)
        def _():
            j = second
            for way in range(2):
                rs_copy(j, 3, way).wait_recv()
            mine_z = ds(z * 128, 128)
            total = part[j, mine_z, :] + rs_in[j, 3, 0].astype(F32) + rs_in[j, 3, 1].astype(F32)
            hid[j, mine_z, :] = (total * slope[j]).astype(BF16)
            for way in range(2):
                hid_copy(j, 0, way).start()

        for s in range(1, 4):
            @when(second - s)
            def _():
                for way in range(2):
                    hid_copy(second - s, s - 1, way).wait_recv()
                    hid_copy(second - s, s, way).start()

        for stage in range(5):
            @pl.when(t == UP_AT[stage])
            def _():
                up_step(stage)

        @pl.when(t == RS_START - 1)
        def _():
            starts[3].wait_recv()

        @when(first + 1)
        def _():
            j = first + 1
            part[j] = dot(up[...], wo[ds(j * WIDTH, WIDTH), :], LAST_LAST)

        j_dw, valid = act_at(t - 4)

        @pl.when(valid)
        def _():
            j = j_dw
            for way in range(2):
                act_copy(j, 3, way).wait_recv()
            for half in range(2):
                dwo[j, half] = dot(act_t[j], up[:, pl.ds(half * HALF, HALF)], PLAIN).astype(BF16)
            here, there = dw_copies(0, j)
            for copy in there:
                copy.start()
            here.start()

        @when(second - 4)
        def _():
            j = second - 4
            for way in range(2):
                hid_copy(j, 3, way).wait_recv()
            for half in range(2):
                dwi[j, half] = dot(inp_t[pl.ds(half * HALF, HALF), :], hid[j], PLAIN).astype(BF16)
            here, there = dw_copies(1, j)
            for copy in there:
                copy.start()
            here.start()

        for stage in range(6):
            @pl.when(t == INP_AT[stage])
            def _():
                inp_step(stage)

        @when(t - INP_AT[5] - 1)
        def _():
            j = t - INP_AT[5] - 1
            for i in range(6 // CHUNKS):
                columns = (j * (6 // CHUNKS) + i) * 128
                inp_t[ds(columns, 128), :] = inp[:, ds(columns, 128)].astype(F32).T.astype(BF16)

        return carry

    lax.fori_loop(0, SLOTS, slot, 0)

    starts[4].wait_recv()

    def sib_copy(i):
        return send(sib_out.at[i], sib_in.at[i], sib_send.at[i], sib_recv.at[i], sibling)

    def partial(i, carry):
        ahead = jnp.where(i == 0, 2, jnp.where(i == 1, 1, jnp.where(i == 2, 3, 0)))
        rows = ds(lax.rem(x + ahead, 4) * 256, 256)
        for half in range(2):
            features = pl.ds(half * HALF, HALF)
            total = dot(hid[0, rows, :], wi[features, pl.ds(0, WIDTH)], LAST_LAST)
            for j in range(1, CHUNKS):
                total += dot(hid[j, rows, :], wi[features, pl.ds(j * WIDTH, WIDTH)], LAST_LAST)
            tail[i, half] = total
        sib_out[i] = tail[i, other].astype(BF16)
        sib_copy(i).start()
        return carry

    lax.fori_loop(0, 4, partial, 0)

    def chip_sum(i, rows):
        return tail[i, core, rows, :] + sib_in[i, rows, :].astype(F32)

    def ends(s, way, size):
        return pl.ds((1 - way if s == 1 else way) * size, size)

    def x_copy(s, way):
        slot, rows = min(s, 1), ends(s, way, 128)
        return send(
            x_out.at[slot, way, rows, :], x_in.at[slot, way, rows, :],
            x_send.at[s, way], x_recv.at[s, way], to_x[way],
        )

    sib_copy(0).wait_recv()
    for way in range(2):
        rows = ends(0, way, 128)
        x_out[0, way, rows, :] = chip_sum(0, rows).astype(BF16)
        x_copy(0, way).start()
    for way in range(2):
        sib_copy(1 + way).wait_recv()
        rows = ends(1, way, 128)
        x_out[1, way, rows, :] = chip_sum(1 + way, rows).astype(BF16)
        x_copy(1, way).start()
    for way in range(2):
        x_copy(0, way).wait_recv()
        rows = ends(2, way, 128)
        x_out[1, way, rows, :] = (chip_sum(1 + way, rows) + x_in[0, way, rows, :].astype(F32)).astype(BF16)
        x_copy(2, way).start()
    sib_copy(3).wait_recv()
    fin[...] = chip_sum(3, pl.ds(0, 256))
    for s in (1, 2):
        for way in range(2):
            x_copy(s, way).wait_recv()
            rows = ends(s, way, 128)
            fin[rows, :] += x_in[1, way, rows, :].astype(F32)

    def y_copy(s, way):
        slot, rows = min(s, 1), ends(s, way, 32)
        return send(
            y_out.at[slot, way, rows, :], y_in.at[slot, way, rows, :],
            y_send.at[s, way], y_recv.at[s, way], to_y[way],
        )

    def fin_rows(ahead, s, way):
        part_at = 32 * (1 - way if s == 1 else way)
        return fin[ds(lax.rem(y + ahead, 4) * 64 + part_at, 32), :]

    for way in range(2):
        y_out[0, way, ends(0, way, 32), :] = fin_rows(2, 0, way).astype(BF16)
        y_copy(0, way).start()
    for way in range(2):
        y_out[1, way, ends(1, way, 32), :] = fin_rows(1 + 2 * way, 1, way).astype(BF16)
        y_copy(1, way).start()
    for way in range(2):
        y_copy(0, way).wait_recv()
        rows = ends(2, way, 32)
        y_out[1, way, rows, :] = (
            fin_rows(1 + 2 * way, 2, way) + y_in[0, way, rows, :].astype(F32)
        ).astype(BF16)
        y_copy(2, way).start()
    for s in (1, 2):
        for way in range(2):
            y_copy(s, way).wait_recv()
    total = fin[ds(y * 64, 64), :] + y_in[1, 0].astype(F32) + y_in[1, 1].astype(F32)
    grad_tokens[...] = total.astype(BF16)

    for copy in (*starts, *up_copies, *inp_copies):
        copy.wait_send()
    for i in range(4):
        sib_copy(i).wait_send()
    for s in range(3):
        for way in range(2):
            x_copy(s, way).wait_send()
            y_copy(s, way).wait_send()

    def drain(j, carry):
        for s in range(4):
            for way in range(2):
                act_copy(j, s, way).wait_send()
                rs_copy(j, s, way).wait_send()
                hid_copy(j, s, way).wait_send()
        for which in range(2):
            here, there = dw_copies(which, j)
            here.wait()
            for copy in there:
                copy.wait()
        return carry

    lax.fori_loop(0, CHUNKS, drain, 0)


def shards(tokens, w_in, w_out, saved, grad_out):
    any_space = pl.BlockSpec(memory_space=pl.ANY)
    vmem = pl.BlockSpec(memory_space=pltpu.VMEM)
    dma = pltpu.SemaphoreType.DMA
    return pl.pallas_call(
        kernel,
        out_shape=(
            jax.ShapeDtypeStruct(tokens.shape, BF16),
            jax.ShapeDtypeStruct(w_in.shape, BF16),
            jax.ShapeDtypeStruct(w_out.shape, BF16),
        ),
        in_specs=[any_space] * 5,
        out_specs=(vmem, any_space, any_space),
        scratch_shapes=[
            pltpu.VMEM((4, 32, QUARTER), BF16),
            pltpu.VMEM((TOKENS, FEATURES), BF16),
            pltpu.VMEM((TOKENS, FEATURES), BF16),
            pltpu.VMEM((FEATURES, TOKENS), BF16),
            pltpu.VMEM((QUARTER, FEATURES), BF16),
            pltpu.VMEM((FEATURES, QUARTER), BF16),
            pltpu.VMEM((CHUNKS, WIDTH, TOKENS), BF16),
            pltpu.VMEM((CHUNKS, TOKENS, WIDTH), BF16),
            pltpu.VMEM((CHUNKS, 128, WIDTH), F32),
            pltpu.VMEM((CHUNKS, TOKENS, WIDTH), F32),
            pltpu.VMEM((CHUNKS, 4, 2, 128, WIDTH), BF16),
            pltpu.VMEM((CHUNKS, 4, 2, 128, WIDTH), BF16),
            pltpu.VMEM((CHUNKS, 2, WIDTH, HALF), BF16),
            pltpu.VMEM((CHUNKS, 2, HALF, WIDTH), BF16),
            pltpu.VMEM((4, 2, 256, HALF), F32),
            pltpu.VMEM((4, 256, HALF), BF16),
            pltpu.VMEM((4, 256, HALF), BF16),
            pltpu.VMEM((2, 2, 256, HALF), BF16),
            pltpu.VMEM((2, 2, 256, HALF), BF16),
            pltpu.VMEM((256, HALF), F32),
            pltpu.VMEM((2, 2, 64, HALF), BF16),
            pltpu.VMEM((2, 2, 64, HALF), BF16),
            dma((5,)),
            dma((5,)), dma((5,)),
            dma((23,)), dma((23,)),
            dma((12,)), dma((12,)),
            dma((CHUNKS, 4, 2)), dma((CHUNKS, 4, 2)),
            dma((CHUNKS, 4, 2)), dma((CHUNKS, 4, 2)),
            dma((CHUNKS, 4, 2)), dma((CHUNKS, 4, 2)),
            dma((2, CHUNKS)), dma((2, CHUNKS, 3)), dma((2, CHUNKS, 3)),
            dma((4,)), dma((4,)),
            dma((3, 2)), dma((3, 2)),
            dma((3, 2)), dma((3, 2)),
        ],
        compiler_params=pltpu.CompilerParams(
            collective_id=0, has_side_effects=True, vmem_limit_bytes=48 * 2**20
        ),
        name="mlp_backward",
    )(tokens, w_in, w_out, saved, grad_out)


def solution(mesh):
    in_specs = (
        P(("depth", "col"), "row"),
        P("row", "col"),
        P("col", "row"),
        P(("depth", "row"), "col"),
        P(("depth", "col"), "row"),
    )
    out_specs = (P(("depth", "col"), "row"), P("row", "col"), P("col", "row"))
    return jax.shard_map(shards, mesh=mesh, in_specs=in_specs, out_specs=out_specs, check_vma=False)
```

```python
import functools
import math

import jax
import jax.numpy as jnp
from jax import lax
from jax.experimental import pallas as pl
from jax.experimental.pallas import tpu as pltpu
from jax.sharding import PartitionSpec as P

F32, BF16 = jnp.float32, jnp.bfloat16
MESH = pl.DeviceIdType.MESH

CHUNKS = 3
QUARTER = 768
WIDTH = QUARTER // CHUNKS
SHARED = (1, 2)
HIDDEN = CHUNKS + len(SHARED)
HALF = 384
FEATURES = 768
TOKENS = 1024

LAST_LAST = (((1,), (1,)), ((), ()))
PLAIN = (((1,), (0,)), ((), ()))


def dot(a, b, dims):
    return lax.dot_general(a, b, dims, preferred_element_type=F32)


def ds(start, size):
    return pl.ds(pl.multiple_of(start, size), size)


def kernel(
    tokens, w_in, w_out, saved, grad_out,
    grad_tokens, grad_w_in, grad_w_out,
    saved_q, up, inp, inp_t, wo, wi, act_t, hid, slope, part,
    rs_out, rs_in, dwo, dwi, tail, sib_out, sib_in,
    x_out, x_in, fin, y_out, y_in,
    local_sem, start_send, start_recv, up_send, up_recv, inp_send, inp_recv,
    act_send, act_recv, rs_send, rs_recv, hid_send, hid_recv,
    dw_local, dw_send, dw_recv, shared_send, shared_recv, sib_send, sib_recv, x_send, x_recv, y_send, y_recv,
):
    depth, row, col = lax.axis_index("depth"), lax.axis_index("row"), lax.axis_index("col")
    z, core = lax.div(row, 2), lax.rem(row, 2)
    x, y_hi = lax.div(col, 2), lax.rem(col, 2)
    y = y_hi * 2 + depth
    other = 1 - core
    quarter = depth * 2 + core

    def at_y(v):
        v = lax.rem(v + 4, 4)
        return (lax.rem(v, 2), row, x * 2 + lax.div(v, 2))

    def at_x(v):
        return (depth, row, lax.rem(v + 4, 4) * 2 + y_hi)

    def at_z(v):
        return (depth, lax.rem(v + 8, 8) * 2 + core, col)

    to_z = (at_z(z + 1), at_z(z - 1))
    to_x = (at_x(x + 1), at_x(x - 1))
    to_y = (at_y(y + 1), at_y(y - 1))
    sibling = (depth, z * 2 + other, col)
    partner = (1 - depth, row, col)
    diagonal = (1 - depth, z * 2 + other, col)

    def send(src, dst, send_sem, recv_sem, device):
        return pltpu.make_async_remote_copy(
            src_ref=src, dst_ref=dst, send_sem=send_sem, recv_sem=recv_sem,
            device_id=device, device_id_type=MESH,
        )

    mine = ds(core * HALF, HALF)

    own_rows = ds(x * 256 + y * 64, 64)
    locals_ = [
        pltpu.make_async_copy(saved.at[:, ds(quarter * QUARTER, QUARTER)], saved_q.at[quarter], local_sem.at[0]),
        pltpu.make_async_copy(grad_out, up.at[own_rows, mine], local_sem.at[1]),
        pltpu.make_async_copy(tokens, inp.at[own_rows, mine], local_sem.at[2]),
        pltpu.make_async_copy(w_out.at[ds(quarter * QUARTER, QUARTER), :], wo.at[:, mine], local_sem.at[3]),
        pltpu.make_async_copy(w_in.at[:, ds(quarter * QUARTER, QUARTER)], wi.at[mine, :], local_sem.at[4]),
    ]
    for copy in locals_:
        copy.start()
    barrier = pltpu.get_barrier_semaphore()
    for device in (*to_z, *to_x, *to_y, sibling, diagonal):
        pl.semaphore_signal(barrier, inc=1, device_id=device, device_id_type=MESH)
    pl.semaphore_wait(barrier, 8)

    sib_quarter = depth * 2 + other
    partner_quarter = (1 - depth) * 2 + core
    starts = []
    for i, (device, q) in enumerate((
        (sibling, sib_quarter),
        (partner, partner_quarter),
        (diagonal, (1 - depth) * 2 + other),
    )):
        starts.append(send(
            saved.at[:, ds(q * QUARTER, QUARTER)], saved_q.at[quarter],
            start_send.at[i], start_recv.at[i], device,
        ))
    starts.append(send(
        w_out.at[ds(sib_quarter * QUARTER, QUARTER), :], wo.at[:, mine],
        start_send.at[3], start_recv.at[3], sibling,
    ))
    starts.append(send(
        w_in.at[:, ds(sib_quarter * QUARTER, QUARTER)], wi.at[mine, :],
        start_send.at[4], start_recv.at[4], sibling,
    ))

    def place(d_x, d_y):
        return lax.rem(x + d_x + 4, 4) * 256 + lax.rem(y + d_y + 4, 4) * 64

    def up_copy(i, rows, size, device, src=None):
        ref = up.at[ds(rows, size), mine]
        return send(ref if src is None else src, ref, up_send.at[i], up_recv.at[i], device)

    up_y = (
        up_copy(0, place(0, 0), 64, to_y[0], grad_out),
        up_copy(1, place(0, 0), 64, to_y[1], grad_out),
        up_copy(2, place(0, -1), 32, to_y[0]),
        up_copy(3, place(0, 1) + 32, 32, to_y[1]),
    )
    steps_y = (0, -1, 1, 2)
    up_x = [
        [
            up_copy(4 + 4 * way + k, place(0, d), 64, to_x[way], grad_out if d == 0 else None)
            for k, d in enumerate(steps_y)
        ]
        for way in range(2)
    ]
    up_far = (
        up_copy(12, place(-1, 0), 64, to_x[0]),
        up_copy(13, place(-1, -1), 64, to_x[0]),
        up_copy(14, place(1, 1), 64, to_x[1]),
        up_copy(15, place(1, 2), 64, to_x[1]),
    )
    up_sib = [
        up_copy(16 + i, lax.rem(x + d + 4, 4) * 256, 256, sibling) for i, d in enumerate((0, -1, 1))
    ] + [up_copy(19 + k, place(2, d), 64, sibling) for k, d in enumerate(steps_y)]
    up_copies = (*up_y, *up_x[0], *up_x[1], *up_far, *up_sib)

    def up_step(stage):
        if stage == 0:
            up_y[0].wait_recv()
            up_y[2].start()
            for way in range(2):
                up_x[way][1].start()
            up_y[1].wait_recv()
            up_y[3].start()
            for way in range(2):
                up_x[way][2].start()
            for way in range(2):
                up_x[way][0].wait_recv()
            up_far[0].start()
        if stage == 1:
            for i in (2, 3):
                up_y[i].wait_recv()
            for way in range(2):
                up_x[way][3].start()
            up_sib[0].start()
            for way in range(2):
                up_x[way][1].wait_recv()
                up_x[way][2].wait_recv()
            up_far[1].start()
            up_far[2].start()
        if stage == 2:
            for way in (1, 0):
                up_x[way][3].wait_recv()
                if way == 1:
                    up_far[3].start()
            up_sib[1].start()
            up_sib[2].start()
            up_far[0].wait_recv()
            up_sib[3].start()
        if stage == 3:
            for k in range(1, 4):
                up_far[k].wait_recv()
                up_sib[3 + k].start()
        if stage == 4:
            for copy in up_sib:
                copy.wait_recv()

    def inp_copy(i, rows, size, device, src=None):
        ref = inp.at[ds(rows, size), mine]
        return send(ref if src is None else src, ref, inp_send.at[i], inp_recv.at[i], device)

    group = lambda d: lax.rem(x + d + 4, 4) * 256
    inp_copies = (
        inp_copy(0, place(0, 0), 64, to_y[0], tokens),
        inp_copy(1, place(0, 0), 64, to_y[1], tokens),
        inp_copy(2, place(0, -1), 32, to_y[0]),
        inp_copy(3, place(0, 1) + 32, 32, to_y[1]),
        inp_copy(4, group(0), 256, to_x[0]),
        inp_copy(5, group(0), 256, to_x[1]),
        inp_copy(6, group(-1), 128, to_x[0]),
        inp_copy(7, group(1) + 128, 128, to_x[1]),
        *[inp_copy(8 + i, group(d), 256, sibling) for i, d in enumerate((0, -1, 1, 2))],
    )

    for copy in starts[:3]:
        copy.start()
    for copy in up_y[:2]:
        copy.start()
    for way in range(2):
        up_x[way][0].start()
    for copy in starts[3:]:
        copy.start()
    for copy in locals_:
        copy.wait()
    for copy in starts[:3]:
        copy.wait_recv()

    def inp_step(stage):
        y0, y1, y2, y3, x0, x1, x2, x3, s0, s1, s2, s3 = inp_copies
        if stage == 0:
            y0.start()
            y1.start()
        if stage == 1:
            y0.wait_recv()
            y2.start()
            y1.wait_recv()
            y3.start()
        if stage == 2:
            y2.wait_recv()
            y3.wait_recv()
            x0.start()
            x1.start()
            s0.start()
        if stage == 3:
            x0.wait_recv()
            x2.start()
            s1.start()
            x1.wait_recv()
            x3.start()
            s2.start()
        if stage == 4:
            x2.wait_recv()
            x3.wait_recv()
            s3.start()
        if stage == 5:
            for copy in (s0, s1, s2, s3):
                copy.wait_recv()

    def act_copy(j, s, way):
        token_block = ds(lax.rem(z + (8 - s if way == 0 else s), 8) * 128, 128)
        if s == 3:
            rows = pl.ds(way * (WIDTH // 2), WIDTH // 2)
        else:
            rows = pl.ds(0, WIDTH)
        ref = act_t.at[j, rows, token_block]
        return send(ref, ref, act_send.at[j, s, way], act_recv.at[j, s, way], to_z[way])

    def hid_copy(j, s, way):
        start = lax.rem(z + (8 - s if way == 0 else s), 8) * 128
        if s == 3:
            ref = hid.at[j, ds(start + way * 64, 64), :]
        else:
            ref = hid.at[j, ds(start, 128), :]
        return send(ref, ref, hid_send.at[j, s, way], hid_recv.at[j, s, way], to_z[way])

    def rs_copy(j, s, way):
        rows = pl.ds(way * 64, 64) if s == 0 else pl.ds(0, 128)
        return send(
            rs_out.at[j, s, way, rows, :], rs_in.at[j, s, way, rows, :],
            rs_send.at[j, s, way], rs_recv.at[j, s, way], to_z[way],
        )

    def dw_copies(which, j):
        if which == 0:
            place = grad_w_out.at[ds(quarter * QUARTER + j * WIDTH, WIDTH), :]
            blocks = dwo
        else:
            of, chunk = (quarter, j) if j < CHUNKS else (partner_quarter, SHARED[j - CHUNKS])
            place = grad_w_in.at[:, ds(of * QUARTER + chunk * WIDTH, WIDTH)]
            blocks = dwi
        here = pltpu.make_async_copy(blocks.at[j, core], place, dw_local.at[which, j])
        targets = ((sibling, other), (partner, core), (diagonal, other))
        if which == 1 and (j >= CHUNKS or j in SHARED):
            targets = targets[:1]
        there = [
            send(blocks.at[j, half], place, dw_send.at[which, j, i], dw_recv.at[which, j, i], device)
            for i, (device, half) in enumerate(targets)
        ]
        return here, there

    def shared_copy(i):
        rows = ds(z * 128, 128)
        return send(
            hid.at[SHARED[i], rows, :], hid.at[CHUNKS + i, rows, :],
            shared_send.at[i], shared_recv.at[i], partner,
        )

    def each(step):
        def body(j, carry):
            step(j)
            return carry

        lax.fori_loop(0, CHUNKS, body, 0)

    def act_first(j):
        values = saved_q[:, :, ds(j * WIDTH, WIDTH)].reshape(128, WIDTH).astype(F32)
        cdf = 0.5 * (1.0 + lax.erf(values / math.sqrt(2.0)))
        pdf = jnp.exp(-0.5 * values * values) / math.sqrt(2.0 * math.pi)
        slope[j] = cdf + values * pdf
        act_t[j, :, ds(z * 128, 128)] = (values * cdf).T.astype(BF16)
        for way in range(2):
            act_copy(j, 0, way).start()

    def act_next(s, j):
        for way in range(2):
            act_copy(j, s - 1, way).wait_recv()
            act_copy(j, s, way).start()

    def rs_first(j):
        part[j] = dot(up[...], wo[ds(j * WIDTH, WIDTH), :], LAST_LAST)
        block = lax.rem(z + 4, 8) * 128
        for way in range(2):
            rows = pl.ds(way * 64, 64)
            rs_out[j, 0, way, rows, :] = part[j, ds(block + way * 64, 64), :].astype(BF16)
            rs_copy(j, 0, way).start()

    def rs_next(s, j):
        for way in range(2):
            rs_copy(j, s - 1, way).wait_recv()
            block = lax.rem(z + (4 - s if way == 0 else 4 + s), 8) * 128
            if s == 1:
                near, far = pl.ds(way * 64, 64), pl.ds((1 - way) * 64, 64)
                rs_out[j, s, way, near, :] = (
                    part[j, ds(block + way * 64, 64), :] + rs_in[j, 0, way, near, :].astype(F32)
                ).astype(BF16)
                rs_out[j, s, way, far, :] = part[j, ds(block + (1 - way) * 64, 64), :].astype(BF16)
            else:
                rs_out[j, s, way] = (
                    part[j, ds(block, 128), :] + rs_in[j, s - 1, way].astype(F32)
                ).astype(BF16)
            rs_copy(j, s, way).start()

    def hid_first(j):
        for way in range(2):
            rs_copy(j, 3, way).wait_recv()
        mine_z = ds(z * 128, 128)
        total = part[j, mine_z, :] + rs_in[j, 3, 0].astype(F32) + rs_in[j, 3, 1].astype(F32)
        hid[j, mine_z, :] = (total * slope[j]).astype(BF16)
        for way in range(2):
            hid_copy(j, 0, way).start()

    def hid_next(s, j):
        for way in range(2):
            hid_copy(j, s - 1, way).wait_recv()
            hid_copy(j, s, way).start()

    def dw_start(which, j):
        here, there = dw_copies(which, j)
        for copy in reversed(there):
            copy.start()
        here.start()

    def dwo_step(j):
        for way in range(2):
            act_copy(j, 3, way).wait_recv()
        for half in range(2):
            dwo[j, half] = dot(act_t[j], up[:, pl.ds(half * HALF, HALF)], PLAIN).astype(BF16)
        dw_start(0, j)

    def hid_last(j):
        for way in range(2):
            hid_copy(j, 3, way).wait_recv()

    def dwi_step(j):
        for half in range(2):
            dwi[j, half] = dot(inp_t[pl.ds(half * HALF, HALF), :], hid[j], PLAIN).astype(BF16)
        dw_start(1, j)

    def turn(first, last):
        def body(b, carry):
            columns = ds(b * 128, 128)
            inp_t[columns, :] = inp[:, columns].astype(F32).T.astype(BF16)
            return carry

        lax.fori_loop(first, last, body, 0)

    each(act_first)
    up_step(0)
    inp_step(0)
    each(functools.partial(act_next, 1))
    up_step(1)
    inp_step(1)
    each(functools.partial(act_next, 2))
    up_step(2)
    inp_step(2)
    each(functools.partial(act_next, 3))
    up_step(3)
    starts[3].wait_recv()
    up_step(4)

    each(rs_first)
    dwo_step(0)
    each(functools.partial(rs_next, 1))
    inp_step(3)
    dwo_step(1)
    each(functools.partial(rs_next, 2))
    inp_step(4)
    dwo_step(2)
    each(functools.partial(rs_next, 3))
    inp_step(5)
    turn(0, 6)

    each(hid_first)
    for i in range(len(SHARED)):
        shared_copy(i).start()
    for s in range(1, 4):
        each(functools.partial(hid_next, s))

    def shared_step(s):
        for i in range(len(SHARED)):
            if s == 0:
                shared_copy(i).wait_recv()
                for way in range(2):
                    hid_copy(CHUNKS + i, 0, way).start()
            elif s < 4:
                hid_next(s, CHUNKS + i)
            else:
                hid_last(CHUNKS + i)
                dwi_step(CHUNKS + i)

    shared_step(0)
    for j in range(CHUNKS):
        hid_last(j)
        if j not in SHARED:
            dwi_step(j)

    starts[4].wait_recv()

    def sib_copy(i):
        return send(sib_out.at[i], sib_in.at[i], sib_send.at[i], sib_recv.at[i], sibling)

    def partial(i, carry):
        ahead = jnp.where(i == 0, 2, jnp.where(i == 1, 1, jnp.where(i == 2, 3, 0)))
        rows = ds(lax.rem(x + ahead, 4) * 256, 256)
        for half in range(2):
            features = pl.ds(half * HALF, HALF)
            total = dot(hid[0, rows, :], wi[features, pl.ds(0, WIDTH)], LAST_LAST)
            for j in range(1, CHUNKS):
                total += dot(hid[j, rows, :], wi[features, pl.ds(j * WIDTH, WIDTH)], LAST_LAST)
            tail[i, half] = total
        sib_out[i] = tail[i, other].astype(BF16)
        sib_copy(i).start()
        return carry

    lax.fori_loop(0, 4, partial, 0)

    def chip_sum(i, rows):
        return tail[i, core, rows, :] + sib_in[i, rows, :].astype(F32)

    def ends(s, way, size):
        return pl.ds((1 - way if s == 1 else way) * size, size)

    def x_copy(s, way):
        slot, rows = min(s, 1), ends(s, way, 128)
        return send(
            x_out.at[slot, way, rows, :], x_in.at[slot, way, rows, :],
            x_send.at[s, way], x_recv.at[s, way], to_x[way],
        )

    sib_copy(0).wait_recv()
    for way in range(2):
        rows = ends(0, way, 128)
        x_out[0, way, rows, :] = chip_sum(0, rows).astype(BF16)
        x_copy(0, way).start()
    for way in range(2):
        sib_copy(1 + way).wait_recv()
        rows = ends(1, way, 128)
        x_out[1, way, rows, :] = chip_sum(1 + way, rows).astype(BF16)
        x_copy(1, way).start()
    shared_step(1)
    for j in SHARED[:1]:
        dwi_step(j)
    for way in range(2):
        x_copy(0, way).wait_recv()
        rows = ends(2, way, 128)
        x_out[1, way, rows, :] = (chip_sum(1 + way, rows) + x_in[0, way, rows, :].astype(F32)).astype(BF16)
        x_copy(2, way).start()
    shared_step(2)
    for j in SHARED[1:]:
        dwi_step(j)
    sib_copy(3).wait_recv()
    fin[...] = chip_sum(3, pl.ds(0, 256))
    for s in (1, 2):
        for way in range(2):
            x_copy(s, way).wait_recv()
            rows = ends(s, way, 128)
            fin[rows, :] += x_in[1, way, rows, :].astype(F32)

    def y_copy(s, way):
        slot, rows = min(s, 1), ends(s, way, 32)
        return send(
            y_out.at[slot, way, rows, :], y_in.at[slot, way, rows, :],
            y_send.at[s, way], y_recv.at[s, way], to_y[way],
        )

    def fin_rows(ahead, s, way):
        part_at = 32 * (1 - way if s == 1 else way)
        return fin[ds(lax.rem(y + ahead, 4) * 64 + part_at, 32), :]

    for way in range(2):
        y_out[0, way, ends(0, way, 32), :] = fin_rows(2, 0, way).astype(BF16)
        y_copy(0, way).start()
    for way in range(2):
        y_out[1, way, ends(1, way, 32), :] = fin_rows(1 + 2 * way, 1, way).astype(BF16)
        y_copy(1, way).start()
    shared_step(3)
    for way in range(2):
        y_copy(0, way).wait_recv()
        rows = ends(2, way, 32)
        y_out[1, way, rows, :] = (
            fin_rows(1 + 2 * way, 2, way) + y_in[0, way, rows, :].astype(F32)
        ).astype(BF16)
        y_copy(2, way).start()
    for s in (1, 2):
        for way in range(2):
            y_copy(s, way).wait_recv()
    total = fin[ds(y * 64, 64), :] + y_in[1, 0].astype(F32) + y_in[1, 1].astype(F32)
    grad_tokens[...] = total.astype(BF16)
    shared_step(4)

    for copy in (*starts, *up_copies, *inp_copies):
        copy.wait_send()
    for i in range(4):
        sib_copy(i).wait_send()
    for s in range(3):
        for way in range(2):
            x_copy(s, way).wait_send()
            y_copy(s, way).wait_send()

    def drain(j, carry):
        for s in range(4):
            for way in range(2):
                act_copy(j, s, way).wait_send()
                rs_copy(j, s, way).wait_send()
                hid_copy(j, s, way).wait_send()
        return carry

    lax.fori_loop(0, CHUNKS, drain, 0)
    for i in range(len(SHARED)):
        shared_copy(i).wait_send()
        for s in range(4):
            for way in range(2):
                hid_copy(CHUNKS + i, s, way).wait_send()
    for which, count in enumerate((CHUNKS, HIDDEN)):
        for j in range(count):
            here, there = dw_copies(which, j)
            here.wait()
            for copy in there:
                copy.wait()


def shards(tokens, w_in, w_out, saved, grad_out):
    any_space = pl.BlockSpec(memory_space=pl.ANY)
    vmem = pl.BlockSpec(memory_space=pltpu.VMEM)
    dma = pltpu.SemaphoreType.DMA
    return pl.pallas_call(
        kernel,
        out_shape=(
            jax.ShapeDtypeStruct(tokens.shape, BF16),
            jax.ShapeDtypeStruct(w_in.shape, BF16),
            jax.ShapeDtypeStruct(w_out.shape, BF16),
        ),
        in_specs=[any_space] * 5,
        out_specs=(vmem, any_space, any_space),
        scratch_shapes=[
            pltpu.VMEM((4, 32, QUARTER), BF16),
            pltpu.VMEM((TOKENS, FEATURES), BF16),
            pltpu.VMEM((TOKENS, FEATURES), BF16),
            pltpu.VMEM((FEATURES, TOKENS), BF16),
            pltpu.VMEM((QUARTER, FEATURES), BF16),
            pltpu.VMEM((FEATURES, QUARTER), BF16),
            pltpu.VMEM((CHUNKS, WIDTH, TOKENS), BF16),
            pltpu.VMEM((HIDDEN, TOKENS, WIDTH), BF16),
            pltpu.VMEM((CHUNKS, 128, WIDTH), F32),
            pltpu.VMEM((CHUNKS, TOKENS, WIDTH), F32),
            pltpu.VMEM((CHUNKS, 4, 2, 128, WIDTH), BF16),
            pltpu.VMEM((CHUNKS, 4, 2, 128, WIDTH), BF16),
            pltpu.VMEM((CHUNKS, 2, WIDTH, HALF), BF16),
            pltpu.VMEM((HIDDEN, 2, HALF, WIDTH), BF16),
            pltpu.VMEM((4, 2, 256, HALF), F32),
            pltpu.VMEM((4, 256, HALF), BF16),
            pltpu.VMEM((4, 256, HALF), BF16),
            pltpu.VMEM((2, 2, 256, HALF), BF16),
            pltpu.VMEM((2, 2, 256, HALF), BF16),
            pltpu.VMEM((256, HALF), F32),
            pltpu.VMEM((2, 2, 64, HALF), BF16),
            pltpu.VMEM((2, 2, 64, HALF), BF16),
            dma((5,)),
            dma((5,)), dma((5,)),
            dma((23,)), dma((23,)),
            dma((12,)), dma((12,)),
            dma((CHUNKS, 4, 2)), dma((CHUNKS, 4, 2)),
            dma((CHUNKS, 4, 2)), dma((CHUNKS, 4, 2)),
            dma((HIDDEN, 4, 2)), dma((HIDDEN, 4, 2)),
            dma((2, HIDDEN)), dma((2, HIDDEN, 3)), dma((2, HIDDEN, 3)),
            dma((len(SHARED),)), dma((len(SHARED),)),
            dma((4,)), dma((4,)),
            dma((3, 2)), dma((3, 2)),
            dma((3, 2)), dma((3, 2)),
        ],
        compiler_params=pltpu.CompilerParams(
            collective_id=0, has_side_effects=True, vmem_limit_bytes=48 * 2**20
        ),
        name="mlp_backward",
    )(tokens, w_in, w_out, saved, grad_out)


def solution(mesh):
    in_specs = (
        P(("depth", "col"), "row"),
        P("row", "col"),
        P("col", "row"),
        P(("depth", "row"), "col"),
        P(("depth", "col"), "row"),
    )
    out_specs = (P(("depth", "col"), "row"), P("row", "col"), P("col", "row"))
    return jax.shard_map(shards, mesh=mesh, in_specs=in_specs, out_specs=out_specs, check_vma=False)
```

```python
import functools
import math

import jax
import jax.numpy as jnp
from jax import lax
from jax.experimental import pallas as pl
from jax.experimental.pallas import tpu as pltpu
from jax.sharding import PartitionSpec as P

F32, BF16 = jnp.float32, jnp.bfloat16
MESH = pl.DeviceIdType.MESH

CHUNKS = 3
QUARTER = 768
WIDTH = QUARTER // CHUNKS
SHARED = (1, 2)
HIDDEN = CHUNKS + len(SHARED)
HALF = 384
FEATURES = 768
TOKENS = 1024

LAST_LAST = (((1,), (1,)), ((), ()))
PLAIN = (((1,), (0,)), ((), ()))


def dot(a, b, dims):
    return lax.dot_general(a, b, dims, preferred_element_type=F32)


def ds(start, size):
    return pl.ds(pl.multiple_of(start, size), size)


def kernel(
    tokens, w_in, w_out, saved, grad_out,
    grad_tokens, grad_w_in, grad_w_out,
    saved_q, up, inp, inp_t, wo, wi, act_t, hid, slope, part,
    rs_out, rs_in, dwo, dwi, tail, sib_out, sib_in,
    x_out, x_in, fin, y_out, y_in,
    local_sem, start_send, start_recv, up_send, up_recv, inp_send, inp_recv,
    act_send, act_recv, rs_send, rs_recv, hid_send, hid_recv,
    dw_local, dw_send, dw_recv, shared_send, shared_recv, sib_send, sib_recv, x_send, x_recv, y_send, y_recv,
):
    depth, row, col = lax.axis_index("depth"), lax.axis_index("row"), lax.axis_index("col")
    z, core = lax.div(row, 2), lax.rem(row, 2)
    x, y_hi = lax.div(col, 2), lax.rem(col, 2)
    y = y_hi * 2 + depth
    other = 1 - core
    quarter = depth * 2 + core

    def at_y(v):
        v = lax.rem(v + 4, 4)
        return (lax.rem(v, 2), row, x * 2 + lax.div(v, 2))

    def at_x(v):
        return (depth, row, lax.rem(v + 4, 4) * 2 + y_hi)

    def at_z(v):
        return (depth, lax.rem(v + 8, 8) * 2 + core, col)

    to_z = (at_z(z + 1), at_z(z - 1))
    to_x = (at_x(x + 1), at_x(x - 1))
    to_y = (at_y(y + 1), at_y(y - 1))
    sibling = (depth, z * 2 + other, col)
    partner = (1 - depth, row, col)
    diagonal = (1 - depth, z * 2 + other, col)

    def send(src, dst, send_sem, recv_sem, device):
        return pltpu.make_async_remote_copy(
            src_ref=src, dst_ref=dst, send_sem=send_sem, recv_sem=recv_sem,
            device_id=device, device_id_type=MESH,
        )

    mine = ds(core * HALF, HALF)

    own_rows = ds(x * 256 + y * 64, 64)
    locals_ = [
        pltpu.make_async_copy(saved.at[:, ds(quarter * QUARTER, QUARTER)], saved_q.at[quarter], local_sem.at[0]),
        pltpu.make_async_copy(grad_out, up.at[own_rows, mine], local_sem.at[1]),
        pltpu.make_async_copy(tokens, inp.at[own_rows, mine], local_sem.at[2]),
        pltpu.make_async_copy(w_out.at[ds(quarter * QUARTER, QUARTER), :], wo.at[:, mine], local_sem.at[3]),
        pltpu.make_async_copy(w_in.at[:, ds(quarter * QUARTER, QUARTER)], wi.at[mine, :], local_sem.at[4]),
    ]
    for copy in locals_:
        copy.start()
    barrier = pltpu.get_barrier_semaphore()
    for device in (*to_z, *to_x, *to_y, at_y(y + 2), sibling, diagonal):
        pl.semaphore_signal(barrier, inc=1, device_id=device, device_id_type=MESH)
    pl.semaphore_wait(barrier, 9)

    sib_quarter = depth * 2 + other
    partner_quarter = (1 - depth) * 2 + core
    starts = []
    for i, (device, q) in enumerate((
        (sibling, sib_quarter),
        (partner, partner_quarter),
        (diagonal, (1 - depth) * 2 + other),
    )):
        starts.append(send(
            saved.at[:, ds(q * QUARTER, QUARTER)], saved_q.at[quarter],
            start_send.at[i], start_recv.at[i], device,
        ))
    starts.append(send(
        w_out.at[ds(sib_quarter * QUARTER, QUARTER), :], wo.at[:, mine],
        start_send.at[3], start_recv.at[3], sibling,
    ))
    starts.append(send(
        w_in.at[:, ds(sib_quarter * QUARTER, QUARTER)], wi.at[mine, :],
        start_send.at[4], start_recv.at[4], sibling,
    ))

    def place(d_x, d_y):
        return lax.rem(x + d_x + 4, 4) * 256 + lax.rem(y + d_y + 4, 4) * 64

    def up_copy(i, rows, size, device, src=None):
        ref = up.at[ds(rows, size), mine]
        return send(ref if src is None else src, ref, up_send.at[i], up_recv.at[i], device)

    up_y = (
        up_copy(0, place(0, 0), 64, to_y[0], grad_out),
        up_copy(1, place(0, 0), 64, to_y[1], grad_out),
        up_copy(2, place(0, -1), 32, to_y[0]),
        up_copy(3, place(0, 1) + 32, 32, to_y[1]),
    )
    steps_y = (0, -1, 1, 2)
    up_x = [
        [
            up_copy(4 + 4 * way + k, place(0, d), 64, to_x[way], grad_out if d == 0 else None)
            for k, d in enumerate(steps_y)
        ]
        for way in range(2)
    ]
    up_far = (
        up_copy(12, place(-1, 0), 64, to_x[0]),
        up_copy(13, place(-1, -1), 64, to_x[0]),
        up_copy(14, place(1, 1), 64, to_x[1]),
        up_copy(15, place(1, 2), 64, to_x[1]),
    )
    up_sib = [
        up_copy(16 + i, lax.rem(x + d + 4, 4) * 256, 256, sibling) for i, d in enumerate((0, -1, 1))
    ] + [up_copy(19 + k, place(2, d), 64, sibling) for k, d in enumerate(steps_y)]
    up_copies = (*up_y, *up_x[0], *up_x[1], *up_far, *up_sib)

    def up_step(stage):
        if stage == 0:
            up_y[0].wait_recv()
            up_y[2].start()
            for way in range(2):
                up_x[way][1].start()
            up_y[1].wait_recv()
            up_y[3].start()
            for way in range(2):
                up_x[way][2].start()
            for way in range(2):
                up_x[way][0].wait_recv()
            up_far[0].start()
        if stage == 1:
            for i in (2, 3):
                up_y[i].wait_recv()
            for way in range(2):
                up_x[way][3].start()
            up_sib[0].start()
            for way in range(2):
                up_x[way][1].wait_recv()
                up_x[way][2].wait_recv()
            up_far[1].start()
            up_far[2].start()
        if stage == 2:
            for way in (1, 0):
                up_x[way][3].wait_recv()
                if way == 1:
                    up_far[3].start()
            up_sib[1].start()
            up_sib[2].start()
            up_far[0].wait_recv()
            up_sib[3].start()
        if stage == 3:
            for k in range(1, 4):
                up_far[k].wait_recv()
                up_sib[3 + k].start()
        if stage == 4:
            for copy in up_sib:
                copy.wait_recv()

    def inp_copy(i, rows, size, device, src=None):
        ref = inp.at[ds(rows, size), mine]
        return send(ref if src is None else src, ref, inp_send.at[i], inp_recv.at[i], device)

    group = lambda d: lax.rem(x + d + 4, 4) * 256
    inp_copies = (
        inp_copy(0, place(0, 0), 64, to_y[0], tokens),
        inp_copy(1, place(0, 0), 64, to_y[1], tokens),
        inp_copy(2, place(0, -1), 32, to_y[0]),
        inp_copy(3, place(0, 1) + 32, 32, to_y[1]),
        inp_copy(4, group(0), 256, to_x[0]),
        inp_copy(5, group(0), 256, to_x[1]),
        inp_copy(6, group(-1), 128, to_x[0]),
        inp_copy(7, group(1) + 128, 128, to_x[1]),
        *[inp_copy(8 + i, group(d), 256, sibling) for i, d in enumerate((0, -1, 1, 2))],
    )

    for copy in starts[:3]:
        copy.start()
    for copy in up_y[:2]:
        copy.start()
    for way in range(2):
        up_x[way][0].start()
    for copy in starts[3:]:
        copy.start()
    for copy in locals_:
        copy.wait()
    for copy in starts[:3]:
        copy.wait_recv()

    def inp_step(stage):
        y0, y1, y2, y3, x0, x1, x2, x3, s0, s1, s2, s3 = inp_copies
        if stage == 0:
            y0.start()
            y1.start()
        if stage == 1:
            y0.wait_recv()
            y2.start()
            y1.wait_recv()
            y3.start()
        if stage == 2:
            y2.wait_recv()
            y3.wait_recv()
            x0.start()
            x1.start()
            s0.start()
        if stage == 3:
            x0.wait_recv()
            x2.start()
            s1.start()
            x1.wait_recv()
            x3.start()
            s2.start()
        if stage == 4:
            x2.wait_recv()
            x3.wait_recv()
            s3.start()
        if stage == 5:
            for copy in (s0, s1, s2, s3):
                copy.wait_recv()

    def act_copy(j, s, way):
        token_block = ds(lax.rem(z + (8 - s if way == 0 else s), 8) * 128, 128)
        if s == 3:
            rows = pl.ds(way * (WIDTH // 2), WIDTH // 2)
        else:
            rows = pl.ds(0, WIDTH)
        ref = act_t.at[j, rows, token_block]
        return send(ref, ref, act_send.at[j, s, way], act_recv.at[j, s, way], to_z[way])

    def hid_copy(j, s, way):
        start = lax.rem(z + (8 - s if way == 0 else s), 8) * 128
        if s == 3:
            ref = hid.at[j, ds(start + way * 64, 64), :]
        else:
            ref = hid.at[j, ds(start, 128), :]
        return send(ref, ref, hid_send.at[j, s, way], hid_recv.at[j, s, way], to_z[way])

    def rs_copy(j, s, way):
        rows = pl.ds(way * 64, 64) if s == 0 else pl.ds(0, 128)
        return send(
            rs_out.at[j, s, way, rows, :], rs_in.at[j, s, way, rows, :],
            rs_send.at[j, s, way], rs_recv.at[j, s, way], to_z[way],
        )

    def dw_copies(which, j):
        if which == 0:
            place = grad_w_out.at[ds(quarter * QUARTER + j * WIDTH, WIDTH), :]
            blocks = dwo
        else:
            of, chunk = (quarter, j) if j < CHUNKS else (partner_quarter, SHARED[j - CHUNKS])
            place = grad_w_in.at[:, ds(of * QUARTER + chunk * WIDTH, WIDTH)]
            blocks = dwi
        here = pltpu.make_async_copy(blocks.at[j, core], place, dw_local.at[which, j])
        targets = ((sibling, other), (partner, core), (diagonal, other))
        if which == 1 and (j >= CHUNKS or j in SHARED):
            targets = targets[:1]
        there = [
            send(blocks.at[j, half], place, dw_send.at[which, j, i], dw_recv.at[which, j, i], device)
            for i, (device, half) in enumerate(targets)
        ]
        return here, there

    def shared_copy(i, ahead, at):
        rows = ds(lax.rem(z + ahead + 8, 8) * 128, 128)
        return send(
            hid.at[SHARED[i], rows, :], hid.at[CHUNKS + i, rows, :],
            shared_send.at[at], shared_recv.at[at], partner,
        )

    again = shared_copy(0, 0, 0)
    across = [shared_copy(1, ahead, 1 + at) for at, ahead in enumerate((0, -1, 1, -2, 2, -3, 3, 4))]

    def each(step):
        def body(j, carry):
            step(j)
            return carry

        lax.fori_loop(0, CHUNKS, body, 0)

    def act_first(j):
        values = saved_q[:, :, ds(j * WIDTH, WIDTH)].reshape(128, WIDTH).astype(F32)
        cdf = 0.5 * (1.0 + lax.erf(values / math.sqrt(2.0)))
        pdf = jnp.exp(-0.5 * values * values) / math.sqrt(2.0 * math.pi)
        slope[j] = cdf + values * pdf
        act_t[j, :, ds(z * 128, 128)] = (values * cdf).T.astype(BF16)
        for way in range(2):
            act_copy(j, 0, way).start()

    def act_next(s, j):
        for way in range(2):
            act_copy(j, s - 1, way).wait_recv()
            act_copy(j, s, way).start()

    def rs_first(j):
        part[j] = dot(up[...], wo[ds(j * WIDTH, WIDTH), :], LAST_LAST)
        block = lax.rem(z + 4, 8) * 128
        for way in range(2):
            rows = pl.ds(way * 64, 64)
            rs_out[j, 0, way, rows, :] = part[j, ds(block + way * 64, 64), :].astype(BF16)
            rs_copy(j, 0, way).start()

    def rs_next(s, j):
        for way in range(2):
            rs_copy(j, s - 1, way).wait_recv()
            block = lax.rem(z + (4 - s if way == 0 else 4 + s), 8) * 128
            if s == 1:
                near, far = pl.ds(way * 64, 64), pl.ds((1 - way) * 64, 64)
                rs_out[j, s, way, near, :] = (
                    part[j, ds(block + way * 64, 64), :] + rs_in[j, 0, way, near, :].astype(F32)
                ).astype(BF16)
                rs_out[j, s, way, far, :] = part[j, ds(block + (1 - way) * 64, 64), :].astype(BF16)
            else:
                rs_out[j, s, way] = (
                    part[j, ds(block, 128), :] + rs_in[j, s - 1, way].astype(F32)
                ).astype(BF16)
            rs_copy(j, s, way).start()

    def hid_first(j):
        for way in range(2):
            rs_copy(j, 3, way).wait_recv()
        mine_z = ds(z * 128, 128)
        total = part[j, mine_z, :] + rs_in[j, 3, 0].astype(F32) + rs_in[j, 3, 1].astype(F32)
        hid[j, mine_z, :] = (total * slope[j]).astype(BF16)
        for way in range(2):
            hid_copy(j, 0, way).start()

    def hid_next(s, j):
        for way in range(2):
            hid_copy(j, s - 1, way).wait_recv()
            hid_copy(j, s, way).start()

    def dw_start(which, j):
        here, there = dw_copies(which, j)
        for copy in reversed(there):
            copy.start()
        here.start()

    def dwo_step(j):
        for way in range(2):
            act_copy(j, 3, way).wait_recv()
        for half in range(2):
            dwo[j, half] = dot(act_t[j], up[:, pl.ds(half * HALF, HALF)], PLAIN).astype(BF16)
        dw_start(0, j)

    def hid_last(j):
        for way in range(2):
            hid_copy(j, 3, way).wait_recv()

    def dwi_step(j):
        for half in range(2):
            dwi[j, half] = dot(inp_t[pl.ds(half * HALF, HALF), :], hid[j], PLAIN).astype(BF16)
        dw_start(1, j)

    def turn(first, last):
        def body(b, carry):
            columns = ds(b * 128, 128)
            inp_t[columns, :] = inp[:, columns].astype(F32).T.astype(BF16)
            return carry

        lax.fori_loop(first, last, body, 0)

    each(act_first)
    up_step(0)
    inp_step(0)
    each(functools.partial(act_next, 1))
    up_step(1)
    inp_step(1)
    each(functools.partial(act_next, 2))
    up_step(2)
    inp_step(2)
    up_step(3)
    each(functools.partial(act_next, 3))
    starts[3].wait_recv()
    up_step(4)

    each(rs_first)
    dwo_step(0)
    each(functools.partial(rs_next, 1))
    inp_step(3)
    dwo_step(1)
    each(functools.partial(rs_next, 2))
    inp_step(4)
    dwo_step(2)
    each(functools.partial(rs_next, 3))
    inp_step(5)
    turn(0, 6)

    each(hid_first)
    again.start()
    across[0].start()
    for s in range(1, 4):
        each(functools.partial(hid_next, s))
        for copy in across[2 * s - 1 : 2 * s + 1]:
            copy.start()

    def shared_step(s):
        if s == 0:
            again.wait_recv()
            for way in range(2):
                hid_copy(CHUNKS, 0, way).start()
        elif s < 4:
            hid_next(s, CHUNKS)
        else:
            hid_last(CHUNKS)
            dwi_step(CHUNKS)

    shared_step(0)
    for j in range(CHUNKS):
        hid_last(j)
    across[7].start()

    starts[4].wait_recv()

    def sib_copy(i):
        return send(sib_out.at[i], sib_in.at[i], sib_send.at[i], sib_recv.at[i], sibling)

    def partial(i, carry):
        ahead = jnp.where(i == 0, 2, jnp.where(i == 1, 1, jnp.where(i == 2, 3, 0)))
        rows = ds(lax.rem(x + ahead, 4) * 256, 256)
        block = jnp.concatenate([hid[j, rows, :] for j in range(CHUNKS)], axis=1)
        for half in range(2):
            tail[i, half] = dot(block, wi[pl.ds(half * HALF, HALF), :], LAST_LAST)
        sib_out[i] = tail[i, other].astype(BF16)
        sib_copy(i).start()
        return carry

    lax.fori_loop(0, 2, partial, 0)

    def chip_sum(i, rows):
        return tail[i, core, rows, :] + sib_in[i, rows, :].astype(F32)

    def ends(s, way, size):
        return pl.ds((1 - way if s == 1 else way) * size, size)

    def x_copy(s, way):
        slot, rows = min(s, 1), ends(s, way, 128)
        return send(
            x_out.at[slot, way, rows, :], x_in.at[slot, way, rows, :],
            x_send.at[s, way], x_recv.at[s, way], to_x[way],
        )

    sib_copy(0).wait_recv()
    for way in range(2):
        rows = ends(0, way, 128)
        x_out[0, way, rows, :] = chip_sum(0, rows).astype(BF16)
        x_copy(0, way).start()
    shared_step(1)
    lax.fori_loop(2, 4, partial, 0)
    for way in range(2):
        sib_copy(1 + way).wait_recv()
        rows = ends(1, way, 128)
        x_out[1, way, rows, :] = chip_sum(1 + way, rows).astype(BF16)
        x_copy(1, way).start()
    dwi_step(0)
    shared_step(2)
    for way in range(2):
        x_copy(0, way).wait_recv()
        rows = ends(2, way, 128)
        x_out[1, way, rows, :] = (chip_sum(1 + way, rows) + x_in[0, way, rows, :].astype(F32)).astype(BF16)
        x_copy(2, way).start()
    dwi_step(1)
    dwi_step(2)
    shared_step(3)
    sib_copy(3).wait_recv()
    fin[...] = chip_sum(3, pl.ds(0, 256))
    for s in (1, 2):
        for way in range(2):
            x_copy(s, way).wait_recv()
            rows = ends(s, way, 128)
            fin[rows, :] += x_in[1, way, rows, :].astype(F32)

    aheads = (2, 1, 3)

    def y_copy(i):
        return send(y_out.at[i], y_in.at[i], y_send.at[i], y_recv.at[i], at_y(y + aheads[i]))

    for i, ahead in enumerate(aheads):
        y_out[i] = fin[ds(lax.rem(y + ahead, 4) * 64, 64), :].astype(BF16)
        y_copy(i).start()
    for copy in across:
        copy.wait_recv()
    dwi_step(CHUNKS + 1)
    shared_step(4)
    total = fin[ds(y * 64, 64), :]
    for i in range(3):
        y_copy(i).wait_recv()
        total += y_in[i].astype(F32)
    grad_tokens[...] = total.astype(BF16)

    for copy in (*starts, *up_copies, *inp_copies):
        copy.wait_send()
    for i in range(4):
        sib_copy(i).wait_send()
    for s in range(3):
        for way in range(2):
            x_copy(s, way).wait_send()
        y_copy(s).wait_send()

    def drain(j, carry):
        for s in range(4):
            for way in range(2):
                act_copy(j, s, way).wait_send()
                rs_copy(j, s, way).wait_send()
                hid_copy(j, s, way).wait_send()
        return carry

    lax.fori_loop(0, CHUNKS, drain, 0)
    for copy in (again, *across):
        copy.wait_send()
    for s in range(4):
        for way in range(2):
            hid_copy(CHUNKS, s, way).wait_send()
    for which, count in enumerate((CHUNKS, HIDDEN)):
        for j in range(count):
            here, there = dw_copies(which, j)
            here.wait()
            for copy in there:
                copy.wait()


def shards(tokens, w_in, w_out, saved, grad_out):
    any_space = pl.BlockSpec(memory_space=pl.ANY)
    vmem = pl.BlockSpec(memory_space=pltpu.VMEM)
    dma = pltpu.SemaphoreType.DMA
    return pl.pallas_call(
        kernel,
        out_shape=(
            jax.ShapeDtypeStruct(tokens.shape, BF16),
            jax.ShapeDtypeStruct(w_in.shape, BF16),
            jax.ShapeDtypeStruct(w_out.shape, BF16),
        ),
        in_specs=[any_space] * 5,
        out_specs=(vmem, any_space, any_space),
        scratch_shapes=[
            pltpu.VMEM((4, 32, QUARTER), BF16),
            pltpu.VMEM((TOKENS, FEATURES), BF16),
            pltpu.VMEM((TOKENS, FEATURES), BF16),
            pltpu.VMEM((FEATURES, TOKENS), BF16),
            pltpu.VMEM((QUARTER, FEATURES), BF16),
            pltpu.VMEM((FEATURES, QUARTER), BF16),
            pltpu.VMEM((CHUNKS, WIDTH, TOKENS), BF16),
            pltpu.VMEM((HIDDEN, TOKENS, WIDTH), BF16),
            pltpu.VMEM((CHUNKS, 128, WIDTH), F32),
            pltpu.VMEM((CHUNKS, TOKENS, WIDTH), F32),
            pltpu.VMEM((CHUNKS, 4, 2, 128, WIDTH), BF16),
            pltpu.VMEM((CHUNKS, 4, 2, 128, WIDTH), BF16),
            pltpu.VMEM((CHUNKS, 2, WIDTH, HALF), BF16),
            pltpu.VMEM((HIDDEN, 2, HALF, WIDTH), BF16),
            pltpu.VMEM((4, 2, 256, HALF), F32),
            pltpu.VMEM((4, 256, HALF), BF16),
            pltpu.VMEM((4, 256, HALF), BF16),
            pltpu.VMEM((2, 2, 256, HALF), BF16),
            pltpu.VMEM((2, 2, 256, HALF), BF16),
            pltpu.VMEM((256, HALF), F32),
            pltpu.VMEM((3, 64, HALF), BF16),
            pltpu.VMEM((3, 64, HALF), BF16),
            dma((5,)),
            dma((5,)), dma((5,)),
            dma((23,)), dma((23,)),
            dma((12,)), dma((12,)),
            dma((CHUNKS, 4, 2)), dma((CHUNKS, 4, 2)),
            dma((CHUNKS, 4, 2)), dma((CHUNKS, 4, 2)),
            dma((HIDDEN, 4, 2)), dma((HIDDEN, 4, 2)),
            dma((2, HIDDEN)), dma((2, HIDDEN, 3)), dma((2, HIDDEN, 3)),
            dma((9,)), dma((9,)),
            dma((4,)), dma((4,)),
            dma((3, 2)), dma((3, 2)),
            dma((3,)), dma((3,)),
        ],
        compiler_params=pltpu.CompilerParams(
            collective_id=0, has_side_effects=True, vmem_limit_bytes=48 * 2**20
        ),
        name="mlp_backward",
    )(tokens, w_in, w_out, saved, grad_out)


def solution(mesh):
    in_specs = (
        P(("depth", "col"), "row"),
        P("row", "col"),
        P("col", "row"),
        P(("depth", "row"), "col"),
        P(("depth", "col"), "row"),
    )
    out_specs = (P(("depth", "col"), "row"), P("row", "col"), P("col", "row"))
    return jax.shard_map(shards, mesh=mesh, in_specs=in_specs, out_specs=out_specs, check_vma=False)
```

```python
import functools
import math

import jax
import jax.numpy as jnp
from jax import lax
from jax.experimental import pallas as pl
from jax.experimental.pallas import tpu as pltpu
from jax.sharding import PartitionSpec as P

F32, BF16 = jnp.float32, jnp.bfloat16
MESH = pl.DeviceIdType.MESH

CHUNKS = 3
QUARTER = 768
WIDTH = QUARTER // CHUNKS
SHARED = (1, 2)
HIDDEN = CHUNKS + len(SHARED)
HALF = 384
FEATURES = 768
TOKENS = 1024

LAST_LAST = (((1,), (1,)), ((), ()))
PLAIN = (((1,), (0,)), ((), ()))


def dot(a, b, dims):
    return lax.dot_general(a, b, dims, preferred_element_type=F32)


def ds(start, size):
    return pl.ds(pl.multiple_of(start, size), size)


def kernel(
    tokens, w_in, w_out, saved, grad_out,
    grad_tokens, grad_w_in, grad_w_out,
    saved_q, up, inp, inp_t, wo, wi, act_t, hid, slope, part,
    rs_out, rs_in, dwo, dwi, tail, sib_out, sib_in,
    x_out, x_in, fin, y_out, y_in,
    local_sem, start_send, start_recv, up_send, up_recv, inp_send, inp_recv,
    act_send, act_recv, rs_send, rs_recv, hid_send, hid_recv,
    dw_local, dw_send, dw_recv, shared_send, shared_recv, sib_send, sib_recv, x_send, x_recv, y_send, y_recv,
):
    depth, row, col = lax.axis_index("depth"), lax.axis_index("row"), lax.axis_index("col")
    z, core = lax.div(row, 2), lax.rem(row, 2)
    x, y_hi = lax.div(col, 2), lax.rem(col, 2)
    y = y_hi * 2 + depth
    other = 1 - core
    quarter = depth * 2 + core

    def at_y(v):
        v = lax.rem(v + 4, 4)
        return (lax.rem(v, 2), row, x * 2 + lax.div(v, 2))

    def at_x(v):
        return (depth, row, lax.rem(v + 4, 4) * 2 + y_hi)

    def at_z(v):
        return (depth, lax.rem(v + 8, 8) * 2 + core, col)

    to_z = (at_z(z + 1), at_z(z - 1))
    to_x = (at_x(x + 1), at_x(x - 1))
    to_y = (at_y(y + 1), at_y(y - 1))
    sibling = (depth, z * 2 + other, col)
    partner = (1 - depth, row, col)
    diagonal = (1 - depth, z * 2 + other, col)

    def send(src, dst, send_sem, recv_sem, device):
        return pltpu.make_async_remote_copy(
            src_ref=src, dst_ref=dst, send_sem=send_sem, recv_sem=recv_sem,
            device_id=device, device_id_type=MESH,
        )

    mine = ds(core * HALF, HALF)

    own_rows = ds(x * 256 + y * 64, 64)
    locals_ = [
        pltpu.make_async_copy(saved.at[:, ds(quarter * QUARTER, QUARTER)], saved_q.at[quarter], local_sem.at[0]),
        pltpu.make_async_copy(grad_out, up.at[own_rows, mine], local_sem.at[1]),
        pltpu.make_async_copy(tokens, inp.at[own_rows, mine], local_sem.at[2]),
        pltpu.make_async_copy(w_out.at[ds(quarter * QUARTER, QUARTER), :], wo.at[:, mine], local_sem.at[3]),
        pltpu.make_async_copy(w_in.at[:, ds(quarter * QUARTER, QUARTER)], wi.at[mine, :], local_sem.at[4]),
    ]
    for copy in locals_:
        copy.start()
    barrier = pltpu.get_barrier_semaphore()
    for device in (*to_z, *to_x, *to_y, at_y(y + 2), sibling, diagonal):
        pl.semaphore_signal(barrier, inc=1, device_id=device, device_id_type=MESH)
    pl.semaphore_wait(barrier, 9)

    sib_quarter = depth * 2 + other
    partner_quarter = (1 - depth) * 2 + core
    starts = []
    for i, (device, q) in enumerate((
        (sibling, sib_quarter),
        (partner, partner_quarter),
        (diagonal, (1 - depth) * 2 + other),
    )):
        starts.append(send(
            saved.at[:, ds(q * QUARTER, QUARTER)], saved_q.at[quarter],
            start_send.at[i], start_recv.at[i], device,
        ))
    starts.append(send(
        w_out.at[ds(sib_quarter * QUARTER, QUARTER), :], wo.at[:, mine],
        start_send.at[3], start_recv.at[3], sibling,
    ))
    starts.append(send(
        w_in.at[:, ds(sib_quarter * QUARTER, QUARTER)], wi.at[mine, :],
        start_send.at[4], start_recv.at[4], sibling,
    ))

    def place(d_x, d_y):
        return lax.rem(x + d_x + 4, 4) * 256 + lax.rem(y + d_y + 4, 4) * 64

    def up_copy(i, rows, size, device, src=None):
        ref = up.at[ds(rows, size), mine]
        return send(ref if src is None else src, ref, up_send.at[i], up_recv.at[i], device)

    up_y = (
        up_copy(0, place(0, 0), 64, to_y[0], grad_out),
        up_copy(1, place(0, 0), 64, to_y[1], grad_out),
        up_copy(2, place(0, -1), 32, to_y[0]),
        up_copy(3, place(0, 1) + 32, 32, to_y[1]),
    )
    steps_y = (0, -1, 1, 2)
    up_x = [
        [
            up_copy(4 + 4 * way + k, place(0, d), 64, to_x[way], grad_out if d == 0 else None)
            for k, d in enumerate(steps_y)
        ]
        for way in range(2)
    ]
    up_far = (
        up_copy(12, place(-1, 0), 64, to_x[0]),
        up_copy(13, place(-1, -1), 64, to_x[0]),
        up_copy(14, place(1, 1), 64, to_x[1]),
        up_copy(15, place(1, 2), 64, to_x[1]),
    )
    up_sib = [
        up_copy(16 + i, lax.rem(x + d + 4, 4) * 256, 256, sibling) for i, d in enumerate((0, -1, 1))
    ] + [up_copy(19 + k, place(2, d), 64, sibling) for k, d in enumerate(steps_y)]
    up_copies = (*up_y, *up_x[0], *up_x[1], *up_far, *up_sib)

    def up_step(stage):
        if stage == 0:
            up_y[0].wait_recv()
            up_y[2].start()
            for way in range(2):
                up_x[way][1].start()
            up_y[1].wait_recv()
            up_y[3].start()
            for way in range(2):
                up_x[way][2].start()
            for way in range(2):
                up_x[way][0].wait_recv()
            up_far[0].start()
        if stage == 1:
            for i in (2, 3):
                up_y[i].wait_recv()
            for way in range(2):
                up_x[way][3].start()
            up_sib[0].start()
            for way in range(2):
                up_x[way][1].wait_recv()
                up_x[way][2].wait_recv()
            up_far[1].start()
            up_far[2].start()
        if stage == 2:
            for way in (1, 0):
                up_x[way][3].wait_recv()
                if way == 1:
                    up_far[3].start()
            up_sib[1].start()
            up_sib[2].start()
            up_far[0].wait_recv()
            up_sib[3].start()
        if stage == 3:
            for k in range(1, 4):
                up_far[k].wait_recv()
                up_sib[3 + k].start()
        if stage == 4:
            for copy in up_sib:
                copy.wait_recv()

    def inp_copy(i, rows, size, device, src=None):
        ref = inp.at[ds(rows, size), mine]
        return send(ref if src is None else src, ref, inp_send.at[i], inp_recv.at[i], device)

    group = lambda d: lax.rem(x + d + 4, 4) * 256
    inp_copies = (
        inp_copy(0, place(0, 0), 64, to_y[0], tokens),
        inp_copy(1, place(0, 0), 64, to_y[1], tokens),
        inp_copy(2, place(0, -1), 32, to_y[0]),
        inp_copy(3, place(0, 1) + 32, 32, to_y[1]),
        inp_copy(4, group(0), 256, to_x[0]),
        inp_copy(5, group(0), 256, to_x[1]),
        inp_copy(6, group(-1), 128, to_x[0]),
        inp_copy(7, group(1) + 128, 128, to_x[1]),
        *[inp_copy(8 + i, group(d), 256, sibling) for i, d in enumerate((0, -1, 1, 2))],
    )

    for copy in starts[:3]:
        copy.start()
    for copy in up_y[:2]:
        copy.start()
    for way in range(2):
        up_x[way][0].start()
    for copy in locals_[:2]:
        copy.wait()
    for copy in starts[:3]:
        copy.wait_recv()

    def inp_step(stage):
        y0, y1, y2, y3, x0, x1, x2, x3, s0, s1, s2, s3 = inp_copies
        if stage == 0:
            y0.start()
            y1.start()
        if stage == 1:
            y0.wait_recv()
            y2.start()
            y1.wait_recv()
            y3.start()
        if stage == 2:
            y2.wait_recv()
            y3.wait_recv()
            x0.start()
            x1.start()
            s0.start()
        if stage == 3:
            x0.wait_recv()
            x2.start()
            s1.start()
            x1.wait_recv()
            x3.start()
            s2.start()
        if stage == 4:
            x2.wait_recv()
            x3.wait_recv()
            s3.start()
        if stage == 5:
            for copy in (s0, s1, s2, s3):
                copy.wait_recv()

    def act_copy(j, s, way):
        token_block = ds(lax.rem(z + (8 - s if way == 0 else s), 8) * 128, 128)
        if s == 3:
            rows = pl.ds(way * (WIDTH // 2), WIDTH // 2)
        else:
            rows = pl.ds(0, WIDTH)
        ref = act_t.at[j, rows, token_block]
        return send(ref, ref, act_send.at[j, s, way], act_recv.at[j, s, way], to_z[way])

    def hid_copy(j, s, way):
        start = lax.rem(z + (8 - s if way == 0 else s), 8) * 128
        if s == 3:
            ref = hid.at[j, ds(start + way * 64, 64), :]
        else:
            ref = hid.at[j, ds(start, 128), :]
        return send(ref, ref, hid_send.at[j, s, way], hid_recv.at[j, s, way], to_z[way])

    def rs_copy(j, s, way):
        rows = pl.ds(way * 64, 64) if s == 0 else pl.ds(0, 128)
        return send(
            rs_out.at[j, s, way, rows, :], rs_in.at[j, s, way, rows, :],
            rs_send.at[j, s, way], rs_recv.at[j, s, way], to_z[way],
        )

    def dw_copies(which, j):
        if which == 0:
            place = grad_w_out.at[ds(quarter * QUARTER + j * WIDTH, WIDTH), :]
            blocks = dwo
        else:
            of, chunk = (quarter, j) if j < CHUNKS else (partner_quarter, SHARED[j - CHUNKS])
            place = grad_w_in.at[:, ds(of * QUARTER + chunk * WIDTH, WIDTH)]
            blocks = dwi
        here = pltpu.make_async_copy(blocks.at[j, core], place, dw_local.at[which, j])
        targets = ((sibling, other), (partner, core), (diagonal, other))
        if which == 1 and (j >= CHUNKS or j in SHARED):
            targets = targets[:1]
        there = [
            send(blocks.at[j, half], place, dw_send.at[which, j, i], dw_recv.at[which, j, i], device)
            for i, (device, half) in enumerate(targets)
        ]
        return here, there

    def shared_copy(i, ahead, at):
        rows = ds(lax.rem(z + ahead + 8, 8) * 128, 128)
        return send(
            hid.at[SHARED[i], rows, :], hid.at[CHUNKS + i, rows, :],
            shared_send.at[at], shared_recv.at[at], partner,
        )

    again = shared_copy(0, 0, 0)
    across = [shared_copy(1, ahead, 1 + at) for at, ahead in enumerate((0, -1, 1, -2, 2, -3, 3, 4))]

    def each(step):
        def body(j, carry):
            step(j)
            return carry

        lax.fori_loop(0, CHUNKS, body, 0)

    def act_first(j):
        values = saved_q[:, :, ds(j * WIDTH, WIDTH)].reshape(128, WIDTH).astype(F32)
        cdf = 0.5 * (1.0 + lax.erf(values / math.sqrt(2.0)))
        pdf = jnp.exp(-0.5 * values * values) / math.sqrt(2.0 * math.pi)
        slope[j] = cdf + values * pdf
        act_t[j, :, ds(z * 128, 128)] = (values * cdf).T.astype(BF16)
        for way in range(2):
            act_copy(j, 0, way).start()

    def act_next(s, j):
        for way in range(2):
            act_copy(j, s - 1, way).wait_recv()
            act_copy(j, s, way).start()

    def rs_first(j):
        part[j] = dot(up[...], wo[ds(j * WIDTH, WIDTH), :], LAST_LAST)
        block = lax.rem(z + 4, 8) * 128
        for way in range(2):
            rows = pl.ds(way * 64, 64)
            rs_out[j, 0, way, rows, :] = part[j, ds(block + way * 64, 64), :].astype(BF16)
            rs_copy(j, 0, way).start()

    def rs_next(s, j):
        for way in range(2):
            rs_copy(j, s - 1, way).wait_recv()
            block = lax.rem(z + (4 - s if way == 0 else 4 + s), 8) * 128
            if s == 1:
                near, far = pl.ds(way * 64, 64), pl.ds((1 - way) * 64, 64)
                rs_out[j, s, way, near, :] = (
                    part[j, ds(block + way * 64, 64), :] + rs_in[j, 0, way, near, :].astype(F32)
                ).astype(BF16)
                rs_out[j, s, way, far, :] = part[j, ds(block + (1 - way) * 64, 64), :].astype(BF16)
            else:
                rs_out[j, s, way] = (
                    part[j, ds(block, 128), :] + rs_in[j, s - 1, way].astype(F32)
                ).astype(BF16)
            rs_copy(j, s, way).start()

    def hid_first(j):
        for way in range(2):
            rs_copy(j, 3, way).wait_recv()
        mine_z = ds(z * 128, 128)
        total = part[j, mine_z, :] + rs_in[j, 3, 0].astype(F32) + rs_in[j, 3, 1].astype(F32)
        hid[j, mine_z, :] = (total * slope[j]).astype(BF16)
        for way in range(2):
            hid_copy(j, 0, way).start()

    def hid_next(s, j):
        for way in range(2):
            hid_copy(j, s - 1, way).wait_recv()
            hid_copy(j, s, way).start()

    def dw_start(which, j):
        here, there = dw_copies(which, j)
        for copy in reversed(there):
            copy.start()
        here.start()

    def dwo_step(j):
        for way in range(2):
            act_copy(j, 3, way).wait_recv()
        for half in range(2):
            dwo[j, half] = dot(act_t[j], up[:, pl.ds(half * HALF, HALF)], PLAIN).astype(BF16)
        dw_start(0, j)

    def hid_last(j):
        for way in range(2):
            hid_copy(j, 3, way).wait_recv()

    def dwi_step(j):
        for half in range(2):
            dwi[j, half] = dot(inp_t[pl.ds(half * HALF, HALF), :], hid[j], PLAIN).astype(BF16)
        dw_start(1, j)

    def turn(first, last):
        def body(b, carry):
            columns = ds(b * 128, 128)
            inp_t[columns, :] = inp[:, columns].astype(F32).T.astype(BF16)
            return carry

        lax.fori_loop(first, last, body, 0)

    each(act_first)
    for copy in starts[3:]:
        copy.start()
    up_step(0)
    each(functools.partial(act_next, 1))
    up_step(1)
    inp_step(0)
    each(functools.partial(act_next, 2))
    up_step(2)
    inp_step(1)
    up_step(3)
    each(functools.partial(act_next, 3))
    starts[3].wait_recv()
    for copy in locals_[2:]:
        copy.wait()
    up_step(4)

    each(rs_first)
    dwo_step(0)
    each(functools.partial(rs_next, 1))
    inp_step(2)
    dwo_step(1)
    each(functools.partial(rs_next, 2))
    inp_step(3)
    dwo_step(2)
    each(functools.partial(rs_next, 3))
    inp_step(4)

    each(hid_first)
    inp_step(5)
    turn(0, 6)
    again.start()
    across[0].start()
    for s in range(1, 4):
        each(functools.partial(hid_next, s))
        for copy in across[2 * s - 1 : 2 * s + 1]:
            copy.start()

    def shared_step(s):
        if s == 0:
            again.wait_recv()
            for way in range(2):
                hid_copy(CHUNKS, 0, way).start()
        elif s < 4:
            hid_next(s, CHUNKS)
        else:
            hid_last(CHUNKS)
            dwi_step(CHUNKS)

    shared_step(0)
    for j in range(CHUNKS):
        hid_last(j)
    across[7].start()

    starts[4].wait_recv()

    def sib_copy(i):
        return send(sib_out.at[i], sib_in.at[i], sib_send.at[i], sib_recv.at[i], sibling)

    def partial(i, carry):
        ahead = jnp.where(i == 0, 2, jnp.where(i == 1, 1, jnp.where(i == 2, 3, 0)))
        rows = ds(lax.rem(x + ahead, 4) * 256, 256)
        block = jnp.concatenate([hid[j, rows, :] for j in range(CHUNKS)], axis=1)
        for half in range(2):
            tail[i, half] = dot(block, wi[pl.ds(half * HALF, HALF), :], LAST_LAST)
        sib_out[i] = tail[i, other].astype(BF16)
        sib_copy(i).start()
        return carry

    lax.fori_loop(0, 2, partial, 0)

    def chip_sum(i, rows):
        return tail[i, core, rows, :] + sib_in[i, rows, :].astype(F32)

    def ends(s, way, size):
        return pl.ds((1 - way if s == 1 else way) * size, size)

    def x_copy(s, way):
        slot, rows = min(s, 1), ends(s, way, 128)
        return send(
            x_out.at[slot, way, rows, :], x_in.at[slot, way, rows, :],
            x_send.at[s, way], x_recv.at[s, way], to_x[way],
        )

    sib_copy(0).wait_recv()
    for way in range(2):
        rows = ends(0, way, 128)
        x_out[0, way, rows, :] = chip_sum(0, rows).astype(BF16)
        x_copy(0, way).start()
    shared_step(1)
    lax.fori_loop(2, 4, partial, 0)
    for way in range(2):
        sib_copy(1 + way).wait_recv()
        rows = ends(1, way, 128)
        x_out[1, way, rows, :] = chip_sum(1 + way, rows).astype(BF16)
        x_copy(1, way).start()
    dwi_step(0)
    shared_step(2)
    for way in range(2):
        x_copy(0, way).wait_recv()
        rows = ends(2, way, 128)
        x_out[1, way, rows, :] = (chip_sum(1 + way, rows) + x_in[0, way, rows, :].astype(F32)).astype(BF16)
        x_copy(2, way).start()
    dwi_step(1)
    dwi_step(2)
    shared_step(3)
    sib_copy(3).wait_recv()
    fin[...] = chip_sum(3, pl.ds(0, 256))
    for s in (1, 2):
        for way in range(2):
            x_copy(s, way).wait_recv()
            rows = ends(s, way, 128)
            fin[rows, :] += x_in[1, way, rows, :].astype(F32)

    aheads = (2, 1, 3)

    def y_copy(i):
        return send(y_out.at[i], y_in.at[i], y_send.at[i], y_recv.at[i], at_y(y + aheads[i]))

    for i, ahead in enumerate(aheads):
        y_out[i] = fin[ds(lax.rem(y + ahead, 4) * 64, 64), :].astype(BF16)
        y_copy(i).start()
    for copy in across:
        copy.wait_recv()
    dwi_step(CHUNKS + 1)
    shared_step(4)
    total = fin[ds(y * 64, 64), :]
    for i in range(3):
        y_copy(i).wait_recv()
        total += y_in[i].astype(F32)
    grad_tokens[...] = total.astype(BF16)

    for copy in (*starts, *up_copies, *inp_copies):
        copy.wait_send()
    for i in range(4):
        sib_copy(i).wait_send()
    for s in range(3):
        for way in range(2):
            x_copy(s, way).wait_send()
        y_copy(s).wait_send()

    def drain(j, carry):
        for s in range(4):
            for way in range(2):
                act_copy(j, s, way).wait_send()
                rs_copy(j, s, way).wait_send()
                hid_copy(j, s, way).wait_send()
        return carry

    lax.fori_loop(0, CHUNKS, drain, 0)
    for copy in (again, *across):
        copy.wait_send()
    for s in range(4):
        for way in range(2):
            hid_copy(CHUNKS, s, way).wait_send()
    for which, count in enumerate((CHUNKS, HIDDEN)):
        for j in range(count):
            here, there = dw_copies(which, j)
            here.wait()
            for copy in there:
                copy.wait()


def shards(tokens, w_in, w_out, saved, grad_out):
    any_space = pl.BlockSpec(memory_space=pl.ANY)
    vmem = pl.BlockSpec(memory_space=pltpu.VMEM)
    dma = pltpu.SemaphoreType.DMA
    return pl.pallas_call(
        kernel,
        out_shape=(
            jax.ShapeDtypeStruct(tokens.shape, BF16),
            jax.ShapeDtypeStruct(w_in.shape, BF16),
            jax.ShapeDtypeStruct(w_out.shape, BF16),
        ),
        in_specs=[any_space] * 5,
        out_specs=(vmem, any_space, any_space),
        scratch_shapes=[
            pltpu.VMEM((4, 32, QUARTER), BF16),
            pltpu.VMEM((TOKENS, FEATURES), BF16),
            pltpu.VMEM((TOKENS, FEATURES), BF16),
            pltpu.VMEM((FEATURES, TOKENS), BF16),
            pltpu.VMEM((QUARTER, FEATURES), BF16),
            pltpu.VMEM((FEATURES, QUARTER), BF16),
            pltpu.VMEM((CHUNKS, WIDTH, TOKENS), BF16),
            pltpu.VMEM((HIDDEN, TOKENS, WIDTH), BF16),
            pltpu.VMEM((CHUNKS, 128, WIDTH), F32),
            pltpu.VMEM((CHUNKS, TOKENS, WIDTH), F32),
            pltpu.VMEM((CHUNKS, 4, 2, 128, WIDTH), BF16),
            pltpu.VMEM((CHUNKS, 4, 2, 128, WIDTH), BF16),
            pltpu.VMEM((CHUNKS, 2, WIDTH, HALF), BF16),
            pltpu.VMEM((HIDDEN, 2, HALF, WIDTH), BF16),
            pltpu.VMEM((4, 2, 256, HALF), F32),
            pltpu.VMEM((4, 256, HALF), BF16),
            pltpu.VMEM((4, 256, HALF), BF16),
            pltpu.VMEM((2, 2, 256, HALF), BF16),
            pltpu.VMEM((2, 2, 256, HALF), BF16),
            pltpu.VMEM((256, HALF), F32),
            pltpu.VMEM((3, 64, HALF), BF16),
            pltpu.VMEM((3, 64, HALF), BF16),
            dma((5,)),
            dma((5,)), dma((5,)),
            dma((23,)), dma((23,)),
            dma((12,)), dma((12,)),
            dma((CHUNKS, 4, 2)), dma((CHUNKS, 4, 2)),
            dma((CHUNKS, 4, 2)), dma((CHUNKS, 4, 2)),
            dma((HIDDEN, 4, 2)), dma((HIDDEN, 4, 2)),
            dma((2, HIDDEN)), dma((2, HIDDEN, 3)), dma((2, HIDDEN, 3)),
            dma((9,)), dma((9,)),
            dma((4,)), dma((4,)),
            dma((3, 2)), dma((3, 2)),
            dma((3,)), dma((3,)),
        ],
        compiler_params=pltpu.CompilerParams(
            collective_id=0, has_side_effects=True, vmem_limit_bytes=48 * 2**20
        ),
        name="mlp_backward",
    )(tokens, w_in, w_out, saved, grad_out)


def solution(mesh):
    in_specs = (
        P(("depth", "col"), "row"),
        P("row", "col"),
        P("col", "row"),
        P(("depth", "row"), "col"),
        P(("depth", "col"), "row"),
    )
    out_specs = (P(("depth", "col"), "row"), P("row", "col"), P("col", "row"))
    return jax.shard_map(shards, mesh=mesh, in_specs=in_specs, out_specs=out_specs, check_vma=False)
```
